128 devices in a mesh: dp: 8 (over z, x_hi), fsdp: 16 (over y, x_lo, core).
Axes of the slice: x: 4 (x_hi: 2, x_lo: 2; x = x_hi * 2 + x_lo), y: 4, z: 4, core: 2. Of those that a mesh axis runs over, the one named last changes fastest.
Arguments:
- old_weight: float32 [8192, 14336], P(('dp', 'fsdp')), may hold values from -6 to 6
- old_first: float32 [8192, 14336], P(('dp', 'fsdp')), may hold values from -2 to 2
- old_second: float32 [8192, 14336], P(('dp', 'fsdp')), may hold values from 0.05 to 2
- tokens: bfloat16 [4096, 8192], P(('dp', 'fsdp')), may hold values from -24 to 24
- cotangent: bfloat16 [4096, 14336], P('dp', 'fsdp'), may hold values from -24 to 24
Outputs:
- new_weight: float32 [8192, 14336], P('dp', 'fsdp')
- new_first: float32 [8192, 14336], P('dp', 'fsdp')
- new_second: float32 [8192, 14336], P('dp', 'fsdp')
- norm_rows: float32 [4096], P(('dp', 'fsdp'))
The draws below stay inside these ranges and needn't reach their ends.
All inputs are finite; a program needn't handle non-finite values.
Results may differ from the reference program's by a relative error of at most 0.019.
Values may be sent and summed in bfloat16 or wider, within the bound.
A program may use at most 128 MiB of HBM per device.

```python
import math
import jax
import jax.numpy as jnp
from jax import lax

D = 8192
FF = 14336
TOK_GRP = 512
TOKENS = 4096
N_DP = 8


def raised(drawn, own_key, source, target, blocks, factor):
    def block_of(position):
        return (jnp.arange(drawn.shape[position]) // (drawn.shape[position] // blocks)).reshape((-1,) + (1,) * (drawn.ndim - 1 - position))

    one_side = jax.random.permutation(own_key, blocks)[block_of(target)]
    far = (block_of(target) + blocks // 2) % blocks
    return jnp.where((block_of(source) == one_side) | (block_of(source) == far), factor * drawn, drawn)


def levels(rng, shape, split, smallest, largest):
    level, own = 1.0, jax.random.fold_in(rng, 6)
    for axis_at, parts in split:
        heights = jnp.exp(jax.random.uniform(jax.random.fold_in(own, axis_at), (parts,), jnp.float32, smallest / len(split), largest / len(split)))
        level = level * jnp.repeat(heights, shape[axis_at] // parts).reshape([-1 if axis == axis_at else 1 for axis in range(len(shape))])
    return level


def noise(own_key, dims, width, reach, pieces=(), kind=jnp.bfloat16):
    factor_of = levels(own_key, dims, pieces, -0.22, 0.18) if pieces else 1.0
    drawn = jax.random.normal(own_key, dims, jnp.float32) * width * factor_of
    return jnp.minimum(jnp.maximum(drawn, -reach), reach).astype(kind)


def bell_draw_with(key, shape, scale, most, cuts, heavy, held_as=jnp.bfloat16):
    result = scale * jax.random.normal(key, shape, jnp.float32)
    if cuts:
        result = result * levels(key, shape, cuts, -0.22, 0.18)
    return jnp.clip(raised(result, jax.random.fold_in(key, 3), *heavy), -most, most).astype(held_as)


def setup_inputs(seed: int = 0) -> dict:
    streams_of = jax.random.split(jax.random.key(seed), 6)
    return {
        "old_weight": noise(streams_of[0], (D, FF), 1.0, 6.0, ((0, 128),), jnp.float32),
        "old_first": noise(streams_of[1], (D, FF), 0.3, 2.0, ((0, 128),), jnp.float32),
        "old_second": jnp.clip(jnp.exp(math.log(2.0) - 3.6888794 * jax.random.uniform(streams_of[2], (D, FF), jnp.float32) ** levels(streams_of[2], (D, FF), ((0, 128),), -0.2, 0.2)), 0.05, 2.0),
        "tokens": bell_draw_with(streams_of[3], (TOKENS, D), 1.0, 24.0, ((0, 128),), (0, 1, 128, 5.5)),
        "cotangent": noise(streams_of[4], (TOKENS, FF), 4.0, 24.0, ((0, 8), (1, 16))),
    }


def reference(old_weight, old_first, old_second, tokens, cotangent):
    fan_scale = D ** (-0.5)
    weight_low = old_weight.astype(jnp.bfloat16)
    preact = jnp.dot(tokens, weight_low, preferred_element_type=jnp.float32) * fan_scale
    gate_sig = jax.nn.sigmoid(preact)
    hidden = preact * gate_sig
    norm_rows = jnp.sqrt(lax.optimization_barrier(jnp.mean(hidden * hidden, axis=1)) + 1e-06)
    slope = (cotangent.astype(jnp.float32) * gate_sig * (1.0 + preact * (1.0 - gate_sig))).astype(jnp.bfloat16)
    token_groups = tokens.reshape(N_DP, TOK_GRP, D)
    slope_groups = slope.reshape(N_DP, TOK_GRP, FF)

    def add_group(total, index):
        group_grad = lax.dot_general(token_groups[index], slope_groups[index], (((0,), (0,)), ((), ())), preferred_element_type=jnp.float32) * fan_scale
        rounded = lax.optimization_barrier(group_grad.astype(jnp.bfloat16))
        return (total + rounded.astype(jnp.float32), None)
    grad, _ = lax.scan(add_group, jnp.zeros((D, FF), jnp.float32), jnp.arange(N_DP, dtype=jnp.int32))
    new_first = 0.9 * old_first + 0.1 * grad
    new_second = 0.95 * old_second + 0.05 * grad * grad
    update = new_first / (1.0 - 0.9 ** 10) / (jnp.sqrt(new_second / (1.0 - 0.95 ** 10)) + 1e-08)
    new_weight = old_weight - 0.02 * (update + 0.1 * old_weight)
    return (new_weight, new_first, new_second, norm_rows)
```

```python
import functools

import jax
import jax.numpy as jnp
from jax import lax
from jax.experimental import pallas as pl
from jax.experimental.pallas import tpu as pltpu
from jax.sharding import PartitionSpec as P

D = 8192
FF = 14336
SCALE = D ** (-0.5)
NF = 16
NZ = 4
GRP = 32
TC = 1024
FC = 896
SR = 64
TOKEN_LEAD = 2
LAG_X, LAG_S, LAG_Z, LAG_G = 2, 3, 4, 6
FIRST_AT, SECOND_AT = 2, 5
MESH = pl.DeviceIdType.MESH
BF, F32 = jnp.bfloat16, jnp.float32


def step_kernel(
    tok, cot, old_w, old_m, old_v,
    out_w, out_m, out_v, out_g, out_n,
    T, W, PS, RR, XO, XS, XR, SL, ACC, ST, CB, NS, NR,
    ld_sem, st_send, st_recv, own_sem, t1_send, t1_recv, tk_send, fw_send, tk_recv,
    rs_send, rs_recv, x_send, x_recv, s_send, s_recv, z_send, z_recv, n_send, n_recv,
):
    d, f = lax.axis_index("dp"), lax.axis_index("fsdp")
    z, xh = lax.div(d, 2), lax.rem(d, 2)
    y, xl, c = lax.div(f, 4), lax.rem(lax.div(f, 2), 2), lax.rem(f, 2)

    def at_f(dy, dxl, dc):
        return lax.rem(y + dy, 4) * 4 + lax.rem(xl + dxl, 2) * 2 + lax.rem(c + dc, 2)

    def piece(s):
        return at_f(lax.div(s, 4), lax.rem(lax.div(s, 2), 2), lax.rem(s, 2))

    def at_d(dz, dxh):
        return lax.rem(z + dz, NZ) * 2 + lax.rem(xh + dxh, 2)

    def remote(src, dst, send, recv, dev):
        return pltpu.make_async_remote_copy(
            src_ref=src, dst_ref=dst, send_sem=send, recv_sem=recv, device_id=dev, device_id_type=MESH
        )

    def rows(start, size):
        return pl.ds(pl.multiple_of(start, 32), size)

    def load(old, k):
        cols = pl.ds(pl.multiple_of(piece(k) * FC, 128), FC)
        return pltpu.make_async_copy(old.at[:, cols], ST.at[k], ld_sem.at[k])

    def load_all(old):
        def go(k, _):
            load(old, k).start()
            return 0

        lax.fori_loop(0, NF, go, 0)

    def state_copy(i, dst, k):
        return remote(
            CB.at[i, k], dst.at[rows(f * SR, SR)], st_send.at[i, k], st_recv.at[i, f], (d, piece(k))
        )

    def state_landed(i, dst, k):
        q = piece(k)
        return remote(CB.at[i, k], dst.at[rows(q * SR, SR)], st_send.at[i, k], st_recv.at[i, q], (d, q))

    def send_state(i, old, dst):
        def go(n, _):
            k = NF - 1 - n
            load(old, k).wait()
            CB[i, k] = ST[k].astype(BF)

            @pl.when(k > 0)
            def _():
                state_copy(i, dst, k).start()

            return 0

        lax.fori_loop(0, NF, go, 0)

    def own_state(i, dst):
        return pltpu.make_async_copy(CB.at[i, 0], dst.at[rows(f * SR, SR)], own_sem.at[i])

    load_all(old_w)

    barrier = pltpu.get_barrier_semaphore()

    def greet_f(k, _):
        pl.semaphore_signal(barrier, inc=1, device_id=(d, piece(k)), device_id_type=MESH)
        return 0

    lax.fori_loop(1, NF, greet_f, 0)

    def greet_d(k, _):
        pl.semaphore_signal(barrier, inc=1, device_id=(lax.rem(d + k, 8), f), device_id_type=MESH)
        return 0

    lax.fori_loop(1, 8, greet_d, 0)
    pl.semaphore_wait(barrier, NF - 1 + 7)

    def t1_copy(k):
        q = lax.rem(d + k, 8)
        cols = pl.ds(pl.multiple_of(q * TC, 128), TC)
        return remote(
            tok.at[:, cols], T.at[f, rows(d * GRP, GRP)], t1_send.at[k], t1_recv.at[d], (q, f)
        )

    def t1_landed(k):
        q = lax.rem(d + k, 8)
        return remote(
            tok.at[:, pl.ds(0, TC)], T.at[f, rows(q * GRP, GRP)], t1_send.at[k], t1_recv.at[q], (q, f)
        )

    def t1_go(k, _):
        t1_copy(k).start()
        return 0

    lax.fori_loop(1, 8, t1_go, 0)
    T[f, rows(d * GRP, GRP)] = tok[:, pl.ds(pl.multiple_of(d * TC, 128), TC)]

    send_state(0, old_w, W)
    own_state(0, W).start()
    load_all(old_m)

    def t1_wait(k, _):
        t1_landed(k).wait_recv()
        return 0

    lax.fori_loop(1, 8, t1_wait, 0)

    def token_copy(q, send, dev_f):
        return remote(T.at[q], T.at[q], send, tk_recv.at[q], (d, dev_f))

    def landed(q):
        return remote(T.at[q], T.at[q], tk_send.at[0], tk_recv.at[q], (d, at_f(0, 0, 1)))

    sibling = at_f(0, 0, 1)
    partner = at_f(0, 1, 0)
    first_sends = [token_copy(f, tk_send.at[0], partner)]
    first_sends += [token_copy(f, tk_send.at[j], at_f(dy, 0, 0)) for j, dy in ((1, 2), (2, 1), (3, 3))]
    first_sends += [token_copy(f, tk_send.at[4], sibling)]
    second_sends = [token_copy(partner, tk_send.at[4 + j], at_f(dy, 0, 0)) for j, dy in ((1, 2), (2, 1), (3, 3))]
    second_sends += [token_copy(partner, tk_send.at[8], sibling)]
    for copy in first_sends:
        copy.start()
    landed(partner).wait_recv()
    for copy in second_sends:
        copy.start()

    own_state(0, W).wait()

    def w_wait(k, _):
        state_landed(0, W, k).wait_recv()
        return 0

    lax.fori_loop(1, NF, w_wait, 0)
    w_out = pltpu.make_async_copy(W, out_w, own_sem.at[3])
    w_out.start()

    ACC[...] = jnp.zeros_like(ACC)

    def rs_copy(s, dz):
        zz = lax.rem(z + dz, NZ)
        return remote(
            PS.at[s, rows(zz * 64, 64)], RR.at[dz - 1, s], rs_send.at[dz - 1, s], rs_recv.at[dz - 1, s],
            (at_d(dz, 0), f),
        )

    def x_copy(s):
        return remote(XS.at[s], XR.at[s], x_send.at[s], x_recv.at[s], (at_d(0, 1), f))

    def s_copy(s):
        mine = SL.at[s, rows(d * GRP, GRP)]
        return remote(mine, mine, s_send.at[s], s_recv.at[s], (at_d(0, 1), f))

    def z_copy(s, dz):
        mine = SL.at[s, rows(z * 64, 64)]
        return remote(mine, mine, z_send.at[dz - 1, s], z_recv.at[dz - 1, s], (at_d(dz, 0), f))

    def n_copy(s):
        return remote(NS.at[s], NR.at[f], n_send.at[s], n_recv.at[f], (d, piece(s)))

    def n_landed(s):
        q = piece(s)
        return remote(NS.at[s], NR.at[q], n_send.at[s], n_recv.at[q], (d, q))

    def tokens_on(j):
        @pl.when((lax.rem(j, 2) == 0) & (j >= 4) & (j < NF))
        def _():
            q = piece(j)
            landed(q).wait_recv()
            token_copy(q, fw_send.at[j], sibling).start()

    def forward(s):
        q = piece(s)

        @pl.when(lax.rem(s, 2) == 1)
        def _():
            landed(q).wait_recv()

        part = jnp.dot(T[q], W[...], preferred_element_type=F32) * SCALE
        PS[s] = part.astype(BF)
        for dz in (2, 1, 3):
            rs_copy(s, dz).start()

    def reduce_z(s):
        for dz in (1, 3, 2):
            rs_copy(s, dz).wait_recv()

        def half(h):
            own = PS[s, rows(z * 64 + h * GRP, GRP)].astype(F32)
            here = rows(h * GRP, GRP)
            return own + RR[0, s, here].astype(F32) + RR[1, s, here].astype(F32) + RR[2, s, here].astype(F32)

        XS[s] = half(1 - xh).astype(BF)
        x_copy(s).start()
        XO[s] = half(xh)

    def slope(s):
        q = piece(s)
        x_copy(s).wait_recv()
        preact = XO[s] + XR[s].astype(F32)
        gate = jax.nn.sigmoid(preact)
        hidden = preact * gate
        cotangent = cot[rows(q * GRP, GRP), :].astype(F32)
        SL[s, rows(d * GRP, GRP)] = (cotangent * gate * (1.0 + preact * (1.0 - gate))).astype(BF)
        s_copy(s).start()
        square = hidden * hidden
        total = square[:, :128]
        for j in range(1, FC // 128):
            total += square[:, j * 128 : (j + 1) * 128]

        @pl.when(s == 0)
        def _():
            NR[f] = total

        @pl.when(s > 0)
        def _():
            NS[s] = total
            n_copy(s).start()

    def spread_z(s):
        s_copy(s).wait_recv()
        for dz in (2, 1, 3):
            z_copy(s, dz).start()

    def gradient(s):
        q = piece(s)
        for dz in (1, 3, 2):
            z_copy(s, dz).wait_recv()

        def tile(m, _):
            here = pl.ds(pl.multiple_of(m * 256, 256), 256)
            ACC[here, :] += lax.dot_general(
                T[q, :, here], SL[s], (((0,), (0,)), ((), ())), preferred_element_type=F32
            )
            return 0

        lax.fori_loop(0, TC // 256, tile, 0)

    def when_in(s, run):
        @pl.when((s >= 0) & (s < NF))
        def _():
            run(s)

    def stage(i, _):
        when_in(i, forward)
        when_in(i - LAG_X, reduce_z)
        when_in(i - LAG_S, slope)
        when_in(i - LAG_Z, spread_z)
        tokens_on(i + TOKEN_LEAD)

        @pl.when(i == FIRST_AT)
        def _():
            send_state(1, old_m, out_m)
            own_state(1, out_m).start()
            load_all(old_v)

        @pl.when(i == SECOND_AT)
        def _():
            send_state(2, old_v, out_v)
            own_state(2, out_v).start()

        when_in(i - LAG_G, gradient)
        return 0

    lax.fori_loop(0, NF + LAG_G, stage, 0)

    g_out = pltpu.make_async_copy(ACC, out_g, own_sem.at[4])
    g_out.start()

    def n_wait(s, total):
        n_landed(s).wait_recv()
        return total + NR[piece(s)]

    square = jnp.sum(lax.fori_loop(1, NF, n_wait, NR[f]), axis=1, keepdims=True)
    out_n[...] = jnp.broadcast_to(jnp.sqrt(square / FF + 1e-06), (GRP, 128))

    for copy in first_sends + second_sends:
        copy.wait_send()
    w_out.wait()
    own_state(1, out_m).wait()
    own_state(2, out_v).wait()

    def t1_end(k, _):
        t1_copy(k).wait_send()
        return 0

    lax.fori_loop(1, 8, t1_end, 0)

    def end(k, _):
        for i, dst in ((0, W), (1, out_m), (2, out_v)):
            state_copy(i, dst, k).wait_send()
        for i, dst in ((1, out_m), (2, out_v)):
            state_landed(i, dst, k).wait_recv()
        n_copy(k).wait_send()
        return 0

    lax.fori_loop(1, NF, end, 0)

    def end_stage(s, _):
        for dz in (1, 2, 3):
            rs_copy(s, dz).wait_send()
            z_copy(s, dz).wait_send()
        x_copy(s).wait_send()
        s_copy(s).wait_send()

        @pl.when((lax.rem(s, 2) == 0) & (s >= 4))
        def _():
            token_copy(piece(s), fw_send.at[s], sibling).wait_send()

        return 0

    lax.fori_loop(0, NF, end_stage, 0)
    g_out.wait()


def update_kernel(w, m, v, g, new_w, new_m, new_v):
    weight, grad = w[...].astype(F32), g[...] * SCALE
    first = 0.9 * m[...].astype(F32) + 0.1 * grad
    second = 0.95 * v[...].astype(F32) + 0.05 * grad * grad
    new_m[...] = first
    new_v[...] = second
    update = first / (1.0 - 0.9**10) / (jnp.sqrt(second / (1.0 - 0.95**10)) + 1e-08)
    new_w[...] = weight - 0.02 * (update + 0.1 * weight)


def body(old_weight, old_first, old_second, tokens, cotangent):
    anywhere = pl.BlockSpec(memory_space=pl.ANY)
    vmem = pl.BlockSpec(memory_space=pltpu.VMEM)
    tile = jax.ShapeDtypeStruct((TC, FC), BF)
    dma = pltpu.SemaphoreType.DMA
    w, m, v, g, n = pl.pallas_call(
        step_kernel,
        out_shape=(
            tile, tile, tile,
            jax.ShapeDtypeStruct((TC, FC), F32),
            jax.ShapeDtypeStruct((GRP, 128), F32),
        ),
        in_specs=[vmem, vmem, anywhere, anywhere, anywhere],
        out_specs=(anywhere, anywhere, anywhere, anywhere, vmem),
        scratch_shapes=[
            pltpu.VMEM((NF, 8 * GRP, TC), BF),
            pltpu.VMEM((TC, FC), BF),
            pltpu.VMEM((NF, 8 * GRP, FC), BF),
            pltpu.VMEM((3, NF, 64, FC), BF),
            pltpu.VMEM((NF, GRP, FC), F32),
            pltpu.VMEM((NF, GRP, FC), BF),
            pltpu.VMEM((NF, GRP, FC), BF),
            pltpu.VMEM((NF, 8 * GRP, FC), BF),
            pltpu.VMEM((TC, FC), F32),
            pltpu.VMEM((NF, SR, FC), F32),
            pltpu.VMEM((3, NF, SR, FC), BF),
            pltpu.VMEM((NF, GRP, 128), F32),
            pltpu.VMEM((NF, GRP, 128), F32),
            dma((NF,)), dma((3, NF)), dma((3, NF)), dma((5,)), dma((8,)), dma((8,)), dma((9,)), dma((NF,)), dma((NF,)),
            dma((3, NF)), dma((3, NF)), dma((NF,)), dma((NF,)), dma((NF,)), dma((NF,)),
            dma((3, NF)), dma((3, NF)), dma((NF,)), dma((NF,)),
        ],
        compiler_params=pltpu.CompilerParams(
            collective_id=1, has_side_effects=True, vmem_limit_bytes=60 << 20
        ),
        name="train_step",
    )(tokens, cotangent, old_weight, old_first, old_second)

    rows = 128
    block = pl.BlockSpec((rows, FC), lambda i: (i, 0))
    shape = jax.ShapeDtypeStruct((TC, FC), F32)
    new_weight, new_first, new_second = pl.pallas_call(
        update_kernel,
        grid=(TC // rows,),
        out_shape=(shape, shape, shape),
        in_specs=[block] * 4,
        out_specs=(block, block, block),
        name="adamw_update",
    )(w, m, v, g)
    return new_weight, new_first, new_second, n[:, 0]


def solution(mesh):
    placed = (
        P(("dp", "fsdp"), None),
        P(("dp", "fsdp"), None),
        P(("dp", "fsdp"), None),
        P(("dp", "fsdp"), None),
        P("dp", "fsdp"),
    )
    return jax.shard_map(
        body,
        mesh=mesh,
        in_specs=placed,
        out_specs=(P("dp", "fsdp"), P("dp", "fsdp"), P("dp", "fsdp"), P(("dp", "fsdp"))),
        check_vma=False,
    )
```

```python
import functools

import jax
import jax.numpy as jnp
from jax import lax
from jax.experimental import pallas as pl
from jax.experimental.pallas import tpu as pltpu
from jax.sharding import PartitionSpec as P

D = 8192
FF = 14336
SCALE = D ** (-0.5)
NF = 16
NZ = 4
UPD_ROWS = 256
GRP = 32
TC = 1024
FC = 896
SR = 64
TOKEN_LEAD = 2
LAGS = (1, 2, 3, 4, 5, 7)
LAG_M, LAG_X, LAG_S, LAG_Z, LAG_H, LAG_G = LAGS
STATES_AT = 6
MESH = pl.DeviceIdType.MESH
BF, F32 = jnp.bfloat16, jnp.float32


def step_kernel(
    tok, cot, old_w, old_m, old_v,
    out_w, out_m, out_v, out_g, out_n,
    T, W, PS, TR, RR, XO, XS, XR, SL, ACC, ST, CB, NS, NR,
    ld_sem, st_send, st_recv, own_sem, t1_send, t1_recv, tk_send, fw_send, tk_recv,
    tr_send, tr_recv, rs_send, rs_recv, x_send, x_recv, s_send, s_recv, z_send, z_recv, n_send, n_recv,
):
    d, f = lax.axis_index("dp"), lax.axis_index("fsdp")
    z, xh = lax.div(d, 2), lax.rem(d, 2)
    y, xl, c = lax.div(f, 4), lax.rem(lax.div(f, 2), 2), lax.rem(f, 2)

    def at_f(dy, dxl, dc):
        return lax.rem(y + dy, 4) * 4 + lax.rem(xl + dxl, 2) * 2 + lax.rem(c + dc, 2)

    def piece(s):
        far = lax.div(jnp.maximum(s - 4, 0), 6)
        near = lax.div(lax.rem(jnp.maximum(s - 4, 0), 6), 2)
        along = 1 + 2 * near - 3 * lax.div(near, 2)
        dy = jnp.where(s < 4, 0, along)
        dxl = jnp.where(s < 4, lax.div(s, 2), far)
        return at_f(dy, dxl, lax.rem(s, 2))

    def at_d(dz, dxh):
        return lax.rem(z + dz, NZ) * 2 + lax.rem(xh + dxh, 2)

    def remote(src, dst, send, recv, dev):
        return pltpu.make_async_remote_copy(
            src_ref=src, dst_ref=dst, send_sem=send, recv_sem=recv, device_id=dev, device_id_type=MESH
        )

    def rows(start, size):
        return pl.ds(pl.multiple_of(start, 32), size)

    def load(old, i, k):
        cols = pl.ds(pl.multiple_of(piece(k) * FC, 128), FC)
        return pltpu.make_async_copy(old.at[:, cols], ST.at[i % 2, k], ld_sem.at[i % 2, k])

    def load_all(old, i):
        def go(n, _):
            load(old, i, NF - 1 - n).start()
            return 0

        lax.fori_loop(0, NF, go, 0)

    def state_copy(i, dst, k):
        return remote(
            CB.at[i, k], dst.at[rows(f * SR, SR)], st_send.at[i, k], st_recv.at[i, f], (d, piece(k))
        )

    def state_landed(i, dst, k):
        q = piece(k)
        return remote(CB.at[i, k], dst.at[rows(q * SR, SR)], st_send.at[i, k], st_recv.at[i, q], (d, q))

    def send_state(i, old, dst, k):
        load(old, i, k).wait()
        CB[i, k] = ST[i % 2, k].astype(BF)

        @pl.when(k > 0)
        def _():
            state_copy(i, dst, k).start()

        @pl.when(k == 0)
        def _():
            own_state(i, dst).start()

    def own_state(i, dst):
        return pltpu.make_async_copy(CB.at[i, 0], dst.at[rows(f * SR, SR)], own_sem.at[i])

    load_all(old_w, 0)
    load_all(old_m, 1)

    barrier = pltpu.get_barrier_semaphore()

    def greet_f(k, _):
        pl.semaphore_signal(barrier, inc=1, device_id=(d, piece(k)), device_id_type=MESH)
        return 0

    lax.fori_loop(1, NF, greet_f, 0)

    def greet_d(k, _):
        pl.semaphore_signal(barrier, inc=1, device_id=(lax.rem(d + k, 8), f), device_id_type=MESH)
        return 0

    lax.fori_loop(1, 8, greet_d, 0)
    pl.semaphore_wait(barrier, NF - 1 + 7)

    def t1_copy(k):
        q = lax.rem(d + k, 8)
        cols = pl.ds(pl.multiple_of(q * TC, 128), TC)
        return remote(
            tok.at[:, cols], T.at[f, rows(d * GRP, GRP)], t1_send.at[k], t1_recv.at[d], (q, f)
        )

    def t1_landed(k):
        q = lax.rem(d + k, 8)
        return remote(
            tok.at[:, pl.ds(0, TC)], T.at[f, rows(q * GRP, GRP)], t1_send.at[k], t1_recv.at[q], (q, f)
        )

    def t1_go(k, _):
        t1_copy(k).start()
        return 0

    lax.fori_loop(1, 8, t1_go, 0)
    T[f, rows(d * GRP, GRP)] = tok[:, pl.ds(pl.multiple_of(d * TC, 128), TC)]

    def w_go(n, _):
        send_state(0, old_w, W, NF - 1 - n)
        return 0

    lax.fori_loop(0, NF, w_go, 0)
    load_all(old_v, 2)

    def t1_wait(k, _):
        t1_landed(k).wait_recv()
        return 0

    lax.fori_loop(1, 8, t1_wait, 0)

    def token_copy(q, send, dev_f):
        return remote(T.at[q], T.at[q], send, tk_recv.at[q], (d, dev_f))

    def landed(q):
        return remote(T.at[q], T.at[q], tk_send.at[0], tk_recv.at[q], (d, at_f(0, 0, 1)))

    sibling = at_f(0, 0, 1)
    partner = at_f(0, 1, 0)
    first_sends = [token_copy(f, tk_send.at[0], partner)]
    first_sends += [token_copy(f, tk_send.at[j], at_f(dy, 0, 0)) for j, dy in ((1, 2), (2, 1), (3, 3))]
    first_sends += [token_copy(f, tk_send.at[4], sibling)]
    second_sends = [token_copy(partner, tk_send.at[4 + j], at_f(dy, 0, 0)) for j, dy in ((1, 2), (2, 1), (3, 3))]
    second_sends += [token_copy(partner, tk_send.at[8], sibling)]
    for copy in first_sends:
        copy.start()
    landed(partner).wait_recv()
    for copy in second_sends:
        copy.start()

    own_state(0, W).wait()

    def w_wait(k, _):
        state_landed(0, W, k).wait_recv()
        return 0

    lax.fori_loop(1, NF, w_wait, 0)
    w_out = pltpu.make_async_copy(W, out_w, own_sem.at[3])
    w_out.start()

    ACC[...] = jnp.zeros_like(ACC)

    def to_z(way):
        return (at_d((1, 3)[way], 0), f)

    def block_z(dz):
        return lax.rem(z + dz, NZ) * 64

    def transit(s, way):
        here = rows(block_z(2) + way * GRP, GRP)
        return remote(PS.at[s, here], TR.at[way, s], tr_send.at[way, s], tr_recv.at[way, s], to_z(way))

    def rs_copy(s, way):
        here = rows(block_z((1, 3)[way]), 64)
        return remote(PS.at[s, here], RR.at[way, s], rs_send.at[way, s], rs_recv.at[way, s], to_z(way))

    def x_copy(s):
        return remote(XS.at[s], XR.at[s], x_send.at[s], x_recv.at[s], (at_d(0, 1), f))

    def s_copy(s):
        mine = SL.at[s, rows(d * GRP, GRP)]
        return remote(mine, mine, s_send.at[s], s_recv.at[s], (at_d(0, 1), f))

    def z_copy(s, way):
        mine = SL.at[s, rows(z * 64, 64)]
        return remote(mine, mine, z_send.at[way, s], z_recv.at[way, s], to_z(way))

    def z_on(s, way):
        here = SL.at[s, rows(block_z((3, 1)[way]) + way * GRP, GRP)]
        return remote(here, here, z_send.at[2 + way, s], z_recv.at[2 + way, s], to_z(way))

    def n_copy(s):
        return remote(NS.at[s], NR.at[f], n_send.at[s], n_recv.at[f], (d, piece(s)))

    def n_landed(s):
        q = piece(s)
        return remote(NS.at[s], NR.at[q], n_send.at[s], n_recv.at[q], (d, q))

    def tokens_on(j):
        @pl.when((lax.rem(j, 2) == 0) & (j >= 4) & (j < NF))
        def _():
            q = piece(j)
            landed(q).wait_recv()
            token_copy(q, fw_send.at[j], sibling).start()

    def forward(s):
        q = piece(s)

        @pl.when(lax.rem(s, 2) == 1)
        def _():
            landed(q).wait_recv()

        part = jnp.dot(T[q], W[...], preferred_element_type=F32) * SCALE
        PS[s] = part.astype(BF)
        for way in (0, 1):
            transit(s, way).start()

    def merge(s):
        for way in (0, 1):
            transit(s, way).wait_recv()
            here = rows(block_z((1, 3)[way]) + way * GRP, GRP)
            PS[s, here] = (PS[s, here].astype(F32) + TR[way, s].astype(F32)).astype(BF)
            rs_copy(s, way).start()

    def reduce_z(s):
        for way in (0, 1):
            rs_copy(s, way).wait_recv()

        def half(h):
            own = PS[s, rows(z * 64 + h * GRP, GRP)].astype(F32)
            here = rows(h * GRP, GRP)
            return own + RR[0, s, here].astype(F32) + RR[1, s, here].astype(F32)

        XS[s] = half(1 - xh).astype(BF)
        x_copy(s).start()
        XO[s] = half(xh)

    def slope(s):
        q = piece(s)
        x_copy(s).wait_recv()
        preact = XO[s] + XR[s].astype(F32)
        gate = jax.nn.sigmoid(preact)
        hidden = preact * gate
        cotangent = cot[rows(q * GRP, GRP), :].astype(F32)
        SL[s, rows(d * GRP, GRP)] = (cotangent * gate * (1.0 + preact * (1.0 - gate))).astype(BF)
        s_copy(s).start()
        square = hidden * hidden
        total = square[:, :128]
        for j in range(1, FC // 128):
            total += square[:, j * 128 : (j + 1) * 128]

        @pl.when(s == 0)
        def _():
            NR[f] = total

        @pl.when(s > 0)
        def _():
            NS[s] = total
            n_copy(s).start()

    def spread_z(s):
        s_copy(s).wait_recv()
        for way in (0, 1):
            z_copy(s, way).start()

    def hand_on(s):
        for way in (0, 1):
            z_copy(s, way).wait_recv()
            z_on(s, way).start()

    def gradient(s):
        q = piece(s)
        for way in (0, 1):
            z_on(s, way).wait_recv()

        def tile(m, _):
            here = pl.ds(pl.multiple_of(m * 256, 256), 256)
            ACC[here, :] += lax.dot_general(
                T[q, :, here], SL[s], (((0,), (0,)), ((), ())), preferred_element_type=F32
            )
            return 0

        lax.fori_loop(0, TC // 256, tile, 0)

    def when_in(s, run):
        @pl.when((s >= 0) & (s < NF))
        def _():
            run(s)

    def stage(i, _):
        when_in(i, forward)
        when_in(i - LAG_M, merge)
        when_in(i - LAG_X, reduce_z)
        when_in(i - LAG_S, slope)
        when_in(i - LAG_Z, spread_z)
        when_in(i - LAG_H, hand_on)
        tokens_on(i + TOKEN_LEAD)

        k = NF - 1 - (i - STATES_AT)

        @pl.when((k >= 0) & (k < NF))
        def _():
            send_state(1, old_m, out_m, k)
            send_state(2, old_v, out_v, k)

        when_in(i - LAG_G, gradient)
        return 0

    lax.fori_loop(0, NF + LAG_G, stage, 0)

    g_out = pltpu.make_async_copy(ACC, out_g, own_sem.at[4])
    g_out.start()

    def n_wait(s, total):
        n_landed(s).wait_recv()
        return total + NR[piece(s)]

    square = jnp.sum(lax.fori_loop(1, NF, n_wait, NR[f]), axis=1, keepdims=True)
    out_n[...] = jnp.broadcast_to(jnp.sqrt(square / FF + 1e-06), (GRP, 128))

    for copy in first_sends + second_sends:
        copy.wait_send()
    w_out.wait()
    own_state(1, out_m).wait()
    own_state(2, out_v).wait()

    def t1_end(k, _):
        t1_copy(k).wait_send()
        return 0

    lax.fori_loop(1, 8, t1_end, 0)

    def end(k, _):
        for i, dst in ((0, W), (1, out_m), (2, out_v)):
            state_copy(i, dst, k).wait_send()
        for i, dst in ((1, out_m), (2, out_v)):
            state_landed(i, dst, k).wait_recv()
        n_copy(k).wait_send()
        return 0

    lax.fori_loop(1, NF, end, 0)

    def end_stage(s, _):
        for way in (0, 1):
            transit(s, way).wait_send()
            rs_copy(s, way).wait_send()
            z_copy(s, way).wait_send()
            z_on(s, way).wait_send()
        x_copy(s).wait_send()
        s_copy(s).wait_send()

        @pl.when((lax.rem(s, 2) == 0) & (s >= 4))
        def _():
            token_copy(piece(s), fw_send.at[s], sibling).wait_send()

        return 0

    lax.fori_loop(0, NF, end_stage, 0)
    g_out.wait()


def update_kernel(w, m, v, g, new_w, new_m, new_v):
    weight, grad = w[...].astype(F32), g[...] * SCALE
    first = 0.9 * m[...].astype(F32) + 0.1 * grad
    second = 0.95 * v[...].astype(F32) + 0.05 * grad * grad
    new_m[...] = first
    new_v[...] = second
    update = first * (1.0 / (1.0 - 0.9**10)) / (jnp.sqrt(second * (1.0 / (1.0 - 0.95**10))) + 1e-08)
    new_w[...] = weight - 0.02 * (update + 0.1 * weight)


def body(old_weight, old_first, old_second, tokens, cotangent):
    anywhere = pl.BlockSpec(memory_space=pl.ANY)
    vmem = pl.BlockSpec(memory_space=pltpu.VMEM)
    tile = jax.ShapeDtypeStruct((TC, FC), BF)
    dma = pltpu.SemaphoreType.DMA
    w, m, v, g, n = pl.pallas_call(
        step_kernel,
        out_shape=(
            tile, tile, tile,
            jax.ShapeDtypeStruct((TC, FC), F32),
            jax.ShapeDtypeStruct((GRP, 128), F32),
        ),
        in_specs=[vmem, vmem, anywhere, anywhere, anywhere],
        out_specs=(anywhere, anywhere, anywhere, anywhere, vmem),
        scratch_shapes=[
            pltpu.VMEM((NF, 8 * GRP, TC), BF),
            pltpu.VMEM((TC, FC), BF),
            pltpu.VMEM((NF, 8 * GRP, FC), BF),
            pltpu.VMEM((2, NF, GRP, FC), BF),
            pltpu.VMEM((2, NF, 64, FC), BF),
            pltpu.VMEM((NF, GRP, FC), F32),
            pltpu.VMEM((NF, GRP, FC), BF),
            pltpu.VMEM((NF, GRP, FC), BF),
            pltpu.VMEM((NF, 8 * GRP, FC), BF),
            pltpu.VMEM((TC, FC), F32),
            pltpu.VMEM((2, NF, SR, FC), F32),
            pltpu.VMEM((3, NF, SR, FC), BF),
            pltpu.VMEM((NF, GRP, 128), F32),
            pltpu.VMEM((NF, GRP, 128), F32),
            dma((2, NF)), dma((3, NF)), dma((3, NF)), dma((5,)), dma((8,)), dma((8,)), dma((9,)), dma((NF,)), dma((NF,)),
            dma((2, NF)), dma((2, NF)), dma((2, NF)), dma((2, NF)), dma((NF,)), dma((NF,)), dma((NF,)), dma((NF,)),
            dma((4, NF)), dma((4, NF)), dma((NF,)), dma((NF,)),
        ],
        compiler_params=pltpu.CompilerParams(
            collective_id=1, has_side_effects=True, vmem_limit_bytes=60 << 20
        ),
        name="train_step",
    )(tokens, cotangent, old_weight, old_first, old_second)

    rows = UPD_ROWS
    block = pl.BlockSpec((rows, FC), lambda i: (i, 0))
    shape = jax.ShapeDtypeStruct((TC, FC), F32)
    new_weight, new_first, new_second = pl.pallas_call(
        update_kernel,
        grid=(TC // rows,),
        out_shape=(shape, shape, shape),
        in_specs=[block] * 4,
        out_specs=(block, block, block),
        name="adamw_update",
    )(w, m, v, g)
    return new_weight, new_first, new_second, n[:, 0]


def solution(mesh):
    placed = (
        P(("dp", "fsdp"), None),
        P(("dp", "fsdp"), None),
        P(("dp", "fsdp"), None),
        P(("dp", "fsdp"), None),
        P("dp", "fsdp"),
    )
    return jax.shard_map(
        body,
        mesh=mesh,
        in_specs=placed,
        out_specs=(P("dp", "fsdp"), P("dp", "fsdp"), P("dp", "fsdp"), P(("dp", "fsdp"))),
        check_vma=False,
    )
```

```python
import functools

import jax
import jax.numpy as jnp
from jax import lax
from jax.experimental import pallas as pl
from jax.experimental.pallas import tpu as pltpu
from jax.sharding import PartitionSpec as P

D = 8192
FF = 14336
SCALE = D ** (-0.5)
NF = 16
NZ = 4
UPD_ROWS = 512
UPD_LIMIT = 60 << 20
GRP = 32
TC = 1024
FC = 896
SR = 64
GROUPS = ((0, 512), (512, 384), (0, 896))
SPLIT = 4
STEPS = NF + SPLIT
TOKEN_LEAD = 2
LAGS = (1, 2, 3, 4, 5, 7)
LAG_M, LAG_X, LAG_S, LAG_Z, LAG_H, LAG_G = LAGS
STATES_AT = 5
MESH = pl.DeviceIdType.MESH
BF, F32 = jnp.bfloat16, jnp.float32


def step_kernel(
    tok, cot, old_w, old_m, old_v,
    out_w, out_m, out_v, out_g, out_n,
    T, W, PS, TR, RR, XO, XS, XR, SL, ACC, ST, CB, NS, NR, COT,
    ld_sem, own_sem, sent, got, tk_recv, tr_recv, rs_recv, x_recv, s_recv, z_recv, on_recv,
):
    d, f = lax.axis_index("dp"), lax.axis_index("fsdp")
    z, xh = lax.div(d, 2), lax.rem(d, 2)
    y, xl, c = lax.div(f, 4), lax.rem(lax.div(f, 2), 2), lax.rem(f, 2)

    def at_f(dy, dxl, dc):
        return lax.rem(y + dy, 4) * 4 + lax.rem(xl + dxl, 2) * 2 + lax.rem(c + dc, 2)

    def piece(s):
        far = lax.div(jnp.maximum(s - 4, 0), 6)
        near = lax.div(lax.rem(jnp.maximum(s - 4, 0), 6), 2)
        along = 1 + 2 * near - 3 * lax.div(near, 2)
        dy = jnp.where(s < 4, 0, along)
        dxl = jnp.where(s < 4, lax.div(s, 2), far)
        return at_f(dy, dxl, lax.rem(s, 2))

    def at_d(dz, dxh):
        return lax.rem(z + dz, NZ) * 2 + lax.rem(xh + dxh, 2)

    def remote(src, dst, send, recv, dev):
        return pltpu.make_async_remote_copy(
            src_ref=src, dst_ref=dst, send_sem=send, recv_sem=recv, device_id=dev, device_id_type=MESH
        )

    def drain(ref, sem):
        pltpu.make_async_copy(ref, ref, sem).wait()

    def rows(start, size):
        return pl.ds(pl.multiple_of(start, 32), size)

    def load(old, i, k):
        cols = pl.ds(pl.multiple_of(piece(k) * FC, 128), FC)
        return pltpu.make_async_copy(old.at[:, cols], ST.at[i % 2, k], ld_sem.at[i])

    def load_all(old, i):
        def go(k, _):
            load(old, i, k).start()
            return 0

        lax.fori_loop(0, NF, go, 0)

    def state_copy(i, dst, k):
        return remote(
            CB.at[i, k], dst.at[rows(f * SR, SR)], sent.at[i], got.at[i], (d, piece(k))
        )

    def w_copy(g, k):
        cols = pl.ds(*GROUPS[g])
        return remote(
            CB.at[0, k, :, cols], W.at[rows(f * SR, SR), cols], sent.at[3 * g], got.at[3 * g], (d, piece(k))
        )

    def w_wait(g):
        drain(W.at[pl.ds(0, (NF - 1) * SR), pl.ds(*GROUPS[g])], got.at[3 * g])

    def state_wait(i, dst):
        drain(dst.at[pl.ds(0, (NF - 1) * SR)], got.at[i])

    def send_state(i, old, dst, k):
        CB[i, k] = ST[i % 2, k].astype(BF)

        @pl.when(k > 0)
        def _():
            state_copy(i, dst, k).start()

        @pl.when(k == 0)
        def _():
            own_state(i, dst).start()

    def own_state(i, dst):
        return pltpu.make_async_copy(CB.at[i, 0], dst.at[rows(f * SR, SR)], own_sem.at[i])

    load_all(old_w, 0)
    own_tokens = pltpu.make_async_copy(
        tok.at[:, pl.ds(pl.multiple_of(d * TC, 128), TC)], T.at[f, rows(d * GRP, GRP)], own_sem.at[0]
    )
    own_tokens.start()
    cot_load = pltpu.make_async_copy(cot, COT, own_sem.at[5])
    cot_load.start()
    load_all(old_m, 1)

    barrier = pltpu.get_barrier_semaphore()

    def greet_f(k, _):
        pl.semaphore_signal(barrier, inc=1, device_id=(d, piece(k)), device_id_type=MESH)
        return 0

    lax.fori_loop(1, NF, greet_f, 0)

    def greet_d(k, _):
        pl.semaphore_signal(barrier, inc=1, device_id=(lax.rem(d + k, 8), f), device_id_type=MESH)
        return 0

    lax.fori_loop(1, 8, greet_d, 0)
    pl.semaphore_wait(barrier, NF - 1 + 7)

    def t1_copy(k):
        q = lax.rem(d + k, 8)
        cols = pl.ds(pl.multiple_of(q * TC, 128), TC)
        return remote(
            tok.at[:, cols], T.at[f, rows(d * GRP, GRP)], sent.at[4], got.at[4], (q, f)
        )

    def t1_go(k, _):
        t1_copy(k).start()
        return 0

    lax.fori_loop(1, 8, t1_go, 0)

    drain(ST.at[0], ld_sem.at[0])

    def w_go(n, _):
        k = NF - 1 - n
        CB[0, k] = ST[0, k].astype(BF)

        @pl.when(k > 0)
        def _():
            w_copy(0, k).start()

        return 0

    lax.fori_loop(0, NF, w_go, 0)
    W[rows(f * SR, SR)] = CB[0, 0]
    load_all(old_v, 2)

    drain(T.at[0, pl.ds(0, 7 * GRP)], got.at[4])
    own_tokens.wait()

    def token_copy(q, dev_f, kind=5):
        return remote(T.at[q], T.at[q], sent.at[kind], tk_recv.at[q], (d, dev_f))

    def landed(q):
        return pltpu.make_async_copy(T.at[q], T.at[q], tk_recv.at[q])

    sibling = at_f(0, 0, 1)
    partner = at_f(0, 1, 0)
    early_sends = [token_copy(f, partner), token_copy(f, sibling)]
    first_sends = [token_copy(f, at_f(dy, 0, 0)) for dy in (1, 3)]
    second_sends = [token_copy(partner, at_f(dy, 0, 0)) for dy in (1, 3)]
    second_sends += [token_copy(partner, sibling)]

    def y_on(dxl):
        return token_copy(at_f(3 - 2 * c, dxl, 0), at_f(1 + 2 * c, 0, 0))

    for copy in early_sends:
        copy.start()
    ACC[...] = jnp.zeros_like(ACC)
    cot_load.wait()
    w_wait(0)

    def w_rest(n, _):
        w_copy(1, NF - 1 - n).start()
        return 0

    lax.fori_loop(0, NF - 1, w_rest, 0)
    for copy in first_sends:
        copy.start()
    w_out = pltpu.make_async_copy(W, out_w, own_sem.at[3])

    def to_z(way):
        return (at_d((1, 3)[way], 0), f)

    def block_z(dz):
        return lax.rem(z + dz, NZ) * 64

    def step_of(g, s):
        return s if g == 0 else s + SPLIT

    def transit(g, s, way):
        here, cols = rows(block_z(2) + way * GRP, GRP), pl.ds(*GROUPS[g])
        return remote(
            PS.at[s, here, cols], TR.at[way, s, :, cols], sent.at[7], tr_recv.at[step_of(g, s)], to_z(way)
        )

    def rs_copy(g, s, way):
        here, cols = rows(block_z((1, 3)[way]), 64), pl.ds(*GROUPS[g])
        return remote(
            PS.at[s, here, cols], RR.at[way, s, :, cols], sent.at[8], rs_recv.at[step_of(g, s)], to_z(way)
        )

    def x_copy(g, s):
        cols = pl.ds(*GROUPS[g])
        return remote(XS.at[s, :, cols], XR.at[s, :, cols], sent.at[9], x_recv.at[step_of(g, s)], (at_d(0, 1), f))

    def s_copy(g, s):
        mine = SL.at[s, rows(d * GRP, GRP), pl.ds(*GROUPS[g])]
        return remote(mine, mine, sent.at[10], s_recv.at[step_of(g, s)], (at_d(0, 1), f))

    def z_copy(g, s, way):
        mine = SL.at[s, rows(z * 64, 64), pl.ds(*GROUPS[g])]
        return remote(mine, mine, sent.at[11], z_recv.at[step_of(g, s)], to_z(way))

    def z_on(g, s, way):
        here = SL.at[s, rows(block_z((3, 1)[way]) + way * GRP, GRP), pl.ds(*GROUPS[g])]
        return remote(here, here, sent.at[12], on_recv.at[step_of(g, s)], to_z(way))

    def n_copy(s):
        return remote(NS.at[s], NR.at[f], sent.at[13], got.at[5], (d, piece(s)))

    def tokens_on(j):
        @pl.when((lax.rem(j, 2) == 0) & (j >= 4) & (j < NF))
        def _():
            q = piece(j)
            landed(q).wait()
            token_copy(q, sibling, 6).start()

        @pl.when(j == 6)
        def _():
            y_on(0).start()

        @pl.when(j == 12)
        def _():
            y_on(1).start()

    def forward(g, s):
        q, cols = piece(s), pl.ds(*GROUPS[g])

        if g != 1:

            @pl.when(lax.rem(s, 2) == 1)
            def _():
                landed(q).wait()
        if g == 1 or SPLIT == 0:

            @pl.when(s == 0)
            def _():
                w_wait(1)
                w_out.start()

        part = jnp.dot(T[q], W[:, cols], preferred_element_type=F32) * SCALE
        PS[s, :, cols] = part.astype(BF)
        for way in (0, 1):
            transit(g, s, way).start()

    def merge(g, s):
        cols = pl.ds(*GROUPS[g])
        drain(TR.at[:, s, :, cols], tr_recv.at[step_of(g, s)])
        for way in (0, 1):
            here = rows(block_z((1, 3)[way]) + way * GRP, GRP)
            PS[s, here, cols] = (PS[s, here, cols].astype(F32) + TR[way, s, :, cols].astype(F32)).astype(BF)
            rs_copy(g, s, way).start()

    def reduce_z(g, s):
        cols = pl.ds(*GROUPS[g])
        drain(RR.at[:, s, :, cols], rs_recv.at[step_of(g, s)])

        def half(h):
            own = PS[s, rows(z * 64 + h * GRP, GRP), cols].astype(F32)
            here = rows(h * GRP, GRP)
            return own + RR[0, s, here, cols].astype(F32) + RR[1, s, here, cols].astype(F32)

        XS[s, :, cols] = half(1 - xh).astype(BF)
        x_copy(g, s).start()
        XO[s, :, cols] = half(xh)

    def slope(g, s):
        q, cols = piece(s), pl.ds(*GROUPS[g])
        x_copy(g, s).wait_recv()
        preact = XO[s, :, cols] + XR[s, :, cols].astype(F32)
        gate = jax.nn.sigmoid(preact)
        hidden = preact * gate
        cotangent = COT[rows(q * GRP, GRP), cols].astype(F32)
        SL[s, rows(d * GRP, GRP), cols] = (cotangent * gate * (1.0 + preact * (1.0 - gate))).astype(BF)
        s_copy(g, s).start()
        square = hidden * hidden
        total = square[:, :128]
        for j in range(1, GROUPS[g][1] // 128):
            total += square[:, j * 128 : (j + 1) * 128]
        if g == 1:
            total += NS[s]
        NS[s] = total
        if g > 0:

            @pl.when(s == 0)
            def _():
                NR[f] = total

            @pl.when(s > 0)
            def _():
                n_copy(s).start()

    def spread_z(g, s):
        s_copy(g, s).wait_recv()
        for way in (0, 1):
            z_copy(g, s, way).start()

    def hand_on(g, s):
        drain(RR.at[:, s, :, pl.ds(*GROUPS[g])], z_recv.at[step_of(g, s)])
        for way in (0, 1):
            z_on(g, s, way).start()

    def gradient(g, s):
        q, cols = piece(s), pl.ds(*GROUPS[g])
        drain(TR.at[:, s, :, cols], on_recv.at[step_of(g, s)])

        def tile(m, _):
            here = pl.ds(pl.multiple_of(m * 256, 256), 256)
            ACC[here, cols] += lax.dot_general(
                T[q, :, here], SL[s, :, cols], (((0,), (0,)), ((), ())), preferred_element_type=F32
            )
            return 0

        lax.fori_loop(0, TC // 256, tile, 0)

    def when_in(i, run):
        for g, first, last, less in ((0, 0, SPLIT, 0), (1, SPLIT, 2 * SPLIT, SPLIT), (2, 2 * SPLIT, STEPS, SPLIT)):

            @pl.when((i >= first) & (i < last))
            def _():
                run(g, i - less)

    def stage(i, _):
        when_in(i, forward)
        when_in(i - LAG_M, merge)
        when_in(i - LAG_X, reduce_z)
        when_in(i - LAG_S, slope)
        when_in(i - LAG_Z, spread_z)
        when_in(i - LAG_H, hand_on)
        tokens_on(i - SPLIT + TOKEN_LEAD)

        @pl.when(i == 0)
        def _():
            landed(partner).wait()
            for copy in second_sends:
                copy.start()

        @pl.when(i == STATES_AT)
        def _():
            drain(ST.at[1], ld_sem.at[1])
            drain(ST.at[0], ld_sem.at[2])

        @pl.when((i >= STATES_AT) & (i < STATES_AT + NF))
        def _():
            n = i - STATES_AT
            for u, old, dst in ((1, old_m, out_m), (2, old_v, out_v)):
                dy, dxl, dc = lax.rem(n + 2 * u + c, 4), lax.rem(lax.div(n, 4) + u, 2), lax.div(n, 8)
                near = jnp.where(dy == 1, 0, jnp.where(dy == 3, 1, 2))
                send_state(u, old, dst, jnp.where(dy == 0, 0, 4 + 4 * dxl + 2 * near) + 2 * dxl + dc)

        when_in(i - LAG_G, gradient)
        return 0

    lax.fori_loop(0, STEPS + LAG_G, stage, 0)

    g_out = pltpu.make_async_copy(ACC, out_g, own_sem.at[4])
    g_out.start()

    drain(NR.at[pl.ds(0, NF - 1)], got.at[5])
    square = jnp.sum(jnp.sum(NR[...], axis=0), axis=1, keepdims=True)
    out_n[...] = jnp.broadcast_to(jnp.sqrt(square / FF + 1e-06), (GRP, 128))

    w_out.wait()
    own_state(1, out_m).wait()
    own_state(2, out_v).wait()
    state_wait(1, out_m)
    state_wait(2, out_v)
    others = pl.ds(0, NF - 1)
    drain(CB.at[0, others, :, pl.ds(*GROUPS[0])], sent.at[0])
    drain(CB.at[1, others], sent.at[1])
    drain(CB.at[2, others], sent.at[2])
    drain(CB.at[0, others, :, pl.ds(*GROUPS[1])], sent.at[3])
    drain(T.at[0, pl.ds(0, 7 * GRP)], sent.at[4])
    drain(T.at[pl.ds(0, 9)], sent.at[5])
    drain(T.at[pl.ds(0, 6)], sent.at[6])
    drain(TR, sent.at[7])
    drain(RR, sent.at[8])
    drain(XS, sent.at[9])
    drain(XS, sent.at[10])
    drain(RR, sent.at[11])
    drain(TR, sent.at[12])
    drain(NS.at[others], sent.at[13])
    g_out.wait()


def update_kernel(w, m, v, g, new_w, new_m, new_v):
    weight, grad = w[...].astype(F32), g[...] * SCALE
    first = 0.9 * m[...].astype(F32) + 0.1 * grad
    second = 0.95 * v[...].astype(F32) + 0.05 * grad * grad
    new_m[...] = first
    new_v[...] = second
    update = first * (1.0 / (1.0 - 0.9**10)) / (jnp.sqrt(second * (1.0 / (1.0 - 0.95**10))) + 1e-08)
    new_w[...] = weight - 0.02 * (update + 0.1 * weight)


def body(old_weight, old_first, old_second, tokens, cotangent):
    anywhere = pl.BlockSpec(memory_space=pl.ANY)
    vmem = pl.BlockSpec(memory_space=pltpu.VMEM)
    tile = jax.ShapeDtypeStruct((TC, FC), BF)
    dma = pltpu.SemaphoreType.DMA
    w, m, v, g, n = pl.pallas_call(
        step_kernel,
        out_shape=(
            tile, tile, tile,
            jax.ShapeDtypeStruct((TC, FC), F32),
            jax.ShapeDtypeStruct((GRP, 128), F32),
        ),
        in_specs=[anywhere] * 5,
        out_specs=(anywhere, anywhere, anywhere, anywhere, vmem),
        scratch_shapes=[
            pltpu.VMEM((NF, 8 * GRP, TC), BF),
            pltpu.VMEM((TC, FC), BF),
            pltpu.VMEM((NF, 8 * GRP, FC), BF),
            pltpu.VMEM((2, NF, GRP, FC), BF),
            pltpu.VMEM((2, NF, 64, FC), BF),
            pltpu.VMEM((NF, GRP, FC), F32),
            pltpu.VMEM((NF, GRP, FC), BF),
            pltpu.VMEM((NF, GRP, FC), BF),
            pltpu.VMEM((NF, 8 * GRP, FC), BF),
            pltpu.VMEM((TC, FC), F32),
            pltpu.VMEM((2, NF, SR, FC), F32),
            pltpu.VMEM((3, NF, SR, FC), BF),
            pltpu.VMEM((NF, GRP, 128), F32),
            pltpu.VMEM((NF, GRP, 128), F32),
            pltpu.VMEM((8 * SR, FC), BF),
            dma((3,)), dma((6,)), dma((14,)), dma((6,)), dma((NF,)),
            dma((STEPS,)), dma((STEPS,)), dma((STEPS,)), dma((STEPS,)), dma((STEPS,)), dma((STEPS,)),
        ],
        compiler_params=pltpu.CompilerParams(
            collective_id=1, has_side_effects=True, vmem_limit_bytes=60 << 20
        ),
        name="train_step",
    )(tokens, cotangent, old_weight, old_first, old_second)

    rows = UPD_ROWS
    block = pl.BlockSpec((rows, FC), lambda i: (i, 0))
    shape = jax.ShapeDtypeStruct((TC, FC), F32)
    new_weight, new_first, new_second = pl.pallas_call(
        update_kernel,
        grid=(TC // rows,),
        out_shape=(shape, shape, shape),
        in_specs=[block] * 4,
        out_specs=(block, block, block),
        compiler_params=pltpu.CompilerParams(vmem_limit_bytes=UPD_LIMIT),
        name="adamw_update",
    )(w, m, v, g)
    return new_weight, new_first, new_second, n[:, 0]


def solution(mesh):
    placed = (
        P(("dp", "fsdp"), None),
        P(("dp", "fsdp"), None),
        P(("dp", "fsdp"), None),
        P(("dp", "fsdp"), None),
        P("dp", "fsdp"),
    )
    return jax.shard_map(
        body,
        mesh=mesh,
        in_specs=placed,
        out_specs=(P("dp", "fsdp"), P("dp", "fsdp"), P("dp", "fsdp"), P(("dp", "fsdp"))),
        check_vma=False,
    )
```

```python
import functools

import jax
import jax.numpy as jnp
from jax import lax
from jax.experimental import pallas as pl
from jax.experimental.pallas import tpu as pltpu
from jax.sharding import PartitionSpec as P

D = 8192
FF = 14336
SCALE = D ** (-0.5)
NF = 16
NZ = 4
UPD_ROWS = 512
UPD_LIMIT = 60 << 20
GRP = 32
TC = 1024
FC = 896
SR = 64
GROUPS = ((0, 512), (512, 384), (0, 896), (0, 896))
SPLIT = 4
STEPS = NF + SPLIT
B_SET = (4, 2)
B_EVERY, B_AT = B_SET
NB = len([s for s in range(SPLIT, NF) if s % B_EVERY == B_AT])
TOKEN_LEAD = 2
LAGS = (1, 2, 3, 4, 5, 7)
LAG_M, LAG_X, LAG_S, LAG_Z, LAG_H, LAG_G = LAGS
STATES_AT = 5
MESH = pl.DeviceIdType.MESH
BF, F32 = jnp.bfloat16, jnp.float32


def step_kernel(
    tok, cot, old_w, old_m, old_v,
    out_w, out_m, out_v, out_g, out_n,
    T, W, PS, TR, RR, XO, XS, XR, XB, SL, ACC, ST, CB, NS, NR, COT,
    ld_sem, own_sem, sent, got, tk_recv, tr_recv, rs_recv, x_recv, s_recv, z_recv, on_recv,
):
    d, f = lax.axis_index("dp"), lax.axis_index("fsdp")
    z, xh = lax.div(d, 2), lax.rem(d, 2)
    y, xl, c = lax.div(f, 4), lax.rem(lax.div(f, 2), 2), lax.rem(f, 2)

    def at_f(dy, dxl, dc):
        return lax.rem(y + dy, 4) * 4 + lax.rem(xl + dxl, 2) * 2 + lax.rem(c + dc, 2)

    def piece(s):
        far = lax.div(jnp.maximum(s - 4, 0), 6)
        near = lax.div(lax.rem(jnp.maximum(s - 4, 0), 6), 2)
        along = 1 + 2 * near - 3 * lax.div(near, 2)
        dy = jnp.where(s < 4, 0, along)
        dxl = jnp.where(s < 4, lax.div(s, 2), far)
        return at_f(dy, dxl, lax.rem(s, 2))

    def at_d(dz, dxh):
        return lax.rem(z + dz, NZ) * 2 + lax.rem(xh + dxh, 2)

    def remote(src, dst, send, recv, dev):
        return pltpu.make_async_remote_copy(
            src_ref=src, dst_ref=dst, send_sem=send, recv_sem=recv, device_id=dev, device_id_type=MESH
        )

    def drain(ref, sem):
        pltpu.make_async_copy(ref, ref, sem).wait()

    def rows(start, size):
        return pl.ds(pl.multiple_of(start, 32), size)

    def load(old, i, k):
        cols = pl.ds(pl.multiple_of(piece(k) * FC, 128), FC)
        return pltpu.make_async_copy(old.at[:, cols], ST.at[i % 2, k], ld_sem.at[i])

    def load_all(old, i):
        def go(k, _):
            load(old, i, k).start()
            return 0

        lax.fori_loop(0, NF, go, 0)

    def state_copy(i, dst, k):
        return remote(
            CB.at[i, k], dst.at[rows(f * SR, SR)], sent.at[i], got.at[i], (d, piece(k))
        )

    def w_copy(g, k):
        cols = pl.ds(*GROUPS[g])
        return remote(
            CB.at[0, k, :, cols], W.at[rows(f * SR, SR), cols], sent.at[3 * g], got.at[3 * g], (d, piece(k))
        )

    def w_wait(g):
        drain(W.at[pl.ds(0, (NF - 1) * SR), pl.ds(*GROUPS[g])], got.at[3 * g])

    def state_wait(i, dst):
        drain(dst.at[pl.ds(0, (NF - 1) * SR)], got.at[i])

    def send_state(i, old, dst, k):
        CB[i, k] = ST[i % 2, k].astype(BF)

        @pl.when(k > 0)
        def _():
            state_copy(i, dst, k).start()

        @pl.when(k == 0)
        def _():
            own_state(i, dst).start()

    def own_state(i, dst):
        return pltpu.make_async_copy(CB.at[i, 0], dst.at[rows(f * SR, SR)], own_sem.at[i])

    load_all(old_w, 0)
    own_tokens = pltpu.make_async_copy(
        tok.at[:, pl.ds(pl.multiple_of(d * TC, 128), TC)], T.at[f, xh, rows(z * GRP, GRP)], own_sem.at[0]
    )
    own_tokens.start()
    cot_load = pltpu.make_async_copy(cot, COT, own_sem.at[5])
    cot_load.start()
    load_all(old_m, 1)

    barrier = pltpu.get_barrier_semaphore()

    def greet_f(k, _):
        pl.semaphore_signal(barrier, inc=1, device_id=(d, piece(k)), device_id_type=MESH)
        return 0

    lax.fori_loop(1, NF, greet_f, 0)

    def greet_d(k, _):
        pl.semaphore_signal(barrier, inc=1, device_id=(lax.rem(d + k, 8), f), device_id_type=MESH)
        return 0

    lax.fori_loop(1, 8, greet_d, 0)
    pl.semaphore_wait(barrier, NF - 1 + 7)

    def t1_copy(k):
        q = lax.rem(d + k, 8)
        cols = pl.ds(pl.multiple_of(q * TC, 128), TC)
        return remote(
            tok.at[:, cols], T.at[f, xh, rows(z * GRP, GRP)], sent.at[4], got.at[4], (q, f)
        )

    def t1_go(k, _):
        t1_copy(k).start()
        return 0

    lax.fori_loop(1, 8, t1_go, 0)

    drain(ST.at[0], ld_sem.at[0])

    def w_go(n, _):
        k = NF - 1 - n
        CB[0, k] = ST[0, k].astype(BF)

        @pl.when(k > 0)
        def _():
            w_copy(0, k).start()

        return 0

    lax.fori_loop(0, NF, w_go, 0)
    W[rows(f * SR, SR)] = CB[0, 0]
    load_all(old_v, 2)

    drain(T.at[0, :, pl.ds(0, 7 * GRP // 2)], got.at[4])
    own_tokens.wait()

    def token_copy(q, dev_f, kind=5):
        return remote(T.at[q], T.at[q], sent.at[kind], tk_recv.at[q], (d, dev_f))

    def landed(q):
        return pltpu.make_async_copy(T.at[q], T.at[q], tk_recv.at[q])

    sibling = at_f(0, 0, 1)
    partner = at_f(0, 1, 0)
    early_sends = [token_copy(f, partner), token_copy(f, sibling)]
    first_sends = [token_copy(f, at_f(dy, 0, 0)) for dy in (1, 3)]
    second_sends = [token_copy(partner, at_f(dy, 0, 0)) for dy in (1, 3)]
    second_sends += [token_copy(partner, sibling)]

    def y_on(dxl):
        return token_copy(at_f(3 - 2 * c, dxl, 0), at_f(1 + 2 * c, 0, 0))

    for copy in early_sends:
        copy.start()
    ACC[...] = jnp.zeros_like(ACC)
    cot_load.wait()
    w_wait(0)

    def w_rest(n, _):
        w_copy(1, NF - 1 - n).start()
        return 0

    lax.fori_loop(0, NF - 1, w_rest, 0)
    for copy in first_sends:
        copy.start()
    w_out = pltpu.make_async_copy(W, out_w, own_sem.at[3])

    def to_z(way):
        return (at_d((1, 3)[way], 0), f)

    def block_z(dz):
        return rows(lax.rem(z + dz, NZ) * GRP, GRP)

    def part_z(dz, way):
        return pl.ds(pl.multiple_of(lax.rem(z + dz, NZ) * GRP + way * 16, 16), 16)

    def step_of(g, s):
        return s if g == 0 else s + SPLIT

    def transit(g, s, way):
        cols = pl.ds(*GROUPS[g])
        return remote(
            PS.at[s, way, block_z(2), cols], TR.at[way, s, :, cols], sent.at[7], tr_recv.at[step_of(g, s)], to_z(way)
        )

    def rs_copy(g, s, way):
        cols = pl.ds(*GROUPS[g])
        return remote(
            PS.at[s, :, block_z((1, 3)[way]), cols], RR.at[way, s, :, :, cols], sent.at[8],
            rs_recv.at[step_of(g, s)], to_z(way),
        )

    def x_copy(g, s):
        cols = pl.ds(*GROUPS[g])
        return remote(XS.at[s, :, cols], XR.at[s, :, cols], sent.at[9], x_recv.at[step_of(g, s)], (at_d(0, 1), f))

    def s_copy(g, s):
        mine = SL.at[s, xh, block_z(0), pl.ds(*GROUPS[g])]
        return remote(mine, mine, sent.at[10], s_recv.at[step_of(g, s)], (at_d(0, 1), f))

    def z_copy(g, s, way):
        mine = SL.at[s, :, block_z(0), pl.ds(*GROUPS[g])]
        return remote(mine, mine, sent.at[11], z_recv.at[step_of(g, s)], to_z(way))

    def z_on(g, s, way):
        here = SL.at[s, way, block_z((3, 1)[way]), pl.ds(*GROUPS[g])]
        return remote(here, here, sent.at[12], on_recv.at[step_of(g, s)], to_z(way))

    def b_cross(s):
        return remote(
            PS.at[s, 1 - xh], XB.at[lax.div(s, B_EVERY)], sent.at[14], tr_recv.at[step_of(3, s)], (at_d(0, 1), f)
        )

    def b_transit(s, way):
        return remote(
            PS.at[s, xh, part_z(2, way)], TR.at[way, s, pl.ds(0, 16)], sent.at[15], rs_recv.at[step_of(3, s)],
            to_z(way),
        )

    def b_rs(s, way):
        return remote(
            PS.at[s, xh, block_z((1, 3)[way])], RR.at[way, s, 0], sent.at[16], x_recv.at[step_of(3, s)], to_z(way)
        )

    def b_z(s, way):
        mine = SL.at[s, xh, block_z(0)]
        return remote(mine, mine, sent.at[17], s_recv.at[step_of(3, s)], to_z(way))

    def b_on(s, way):
        here = SL.at[s, xh, part_z((3, 1)[way], way)]
        return remote(here, here, sent.at[18], z_recv.at[step_of(3, s)], to_z(way))

    def b_back(s):
        mine = SL.at[s, xh]
        return remote(mine, mine, sent.at[19], on_recv.at[step_of(3, s)], (at_d(0, 1), f))

    def n_copy(s):
        return remote(NS.at[s], NR.at[f], sent.at[13], got.at[5], (d, piece(s)))

    def tokens_on(j):
        @pl.when((lax.rem(j, 2) == 0) & (j >= 4) & (j < NF))
        def _():
            q = piece(j)
            landed(q).wait()
            token_copy(q, sibling, 6).start()

        @pl.when(j == 6)
        def _():
            y_on(0).start()

        @pl.when(j == 12)
        def _():
            y_on(1).start()

    def forward(g, s):
        q, cols = piece(s), pl.ds(*GROUPS[g])

        if g != 1:

            @pl.when(lax.rem(s, 2) == 1)
            def _():
                landed(q).wait()
        if g == 1 or SPLIT == 0:

            @pl.when(s == 0)
            def _():
                w_wait(1)
                w_out.start()

        part = jnp.dot(T[q].reshape(8 * GRP, TC), W[:, cols], preferred_element_type=F32) * SCALE
        PS[s, :, :, cols] = part.astype(BF).reshape(2, 4 * GRP, GROUPS[g][1])
        if g == 3:
            b_cross(s).start()
        else:
            for way in (0, 1):
                transit(g, s, way).start()

    def b_merge(g, s):
        drain(XB.at[0], tr_recv.at[step_of(3, s)])
        PS[s, xh] = (PS[s, xh].astype(F32) + XB[lax.div(s, B_EVERY)].astype(F32)).astype(BF)
        for way in (0, 1):
            b_transit(s, way).start()

    def b_reduce(g, s):
        drain(TR.at[:, s, pl.ds(0, 16)], rs_recv.at[step_of(3, s)])
        for way in (0, 1):
            here = part_z((1, 3)[way], way)
            PS[s, xh, here] = (PS[s, xh, here].astype(F32) + TR[way, s, pl.ds(0, 16)].astype(F32)).astype(BF)
            b_rs(s, way).start()

    def b_slope(g, s):
        drain(TR.at[:, s], x_recv.at[step_of(3, s)])
        preact = PS[s, xh, block_z(0)].astype(F32) + RR[0, s, 0].astype(F32) + RR[1, s, 0].astype(F32)
        slope_of(g, s, preact)
        for way in (0, 1):
            b_z(s, way).start()

    def b_spread(g, s):
        drain(TR.at[:, s], s_recv.at[step_of(3, s)])
        for way in (0, 1):
            b_on(s, way).start()

    def b_hand(g, s):
        drain(TR.at[:, s, pl.ds(0, 16)], z_recv.at[step_of(3, s)])
        b_back(s).start()

    def merge(g, s):
        cols = pl.ds(*GROUPS[g])
        drain(TR.at[:, s, :, cols], tr_recv.at[step_of(g, s)])
        for way in (0, 1):
            here = block_z((1, 3)[way])
            PS[s, way, here, cols] = (PS[s, way, here, cols].astype(F32) + TR[way, s, :, cols].astype(F32)).astype(BF)
            rs_copy(g, s, way).start()

    def reduce_z(g, s):
        cols = pl.ds(*GROUPS[g])
        drain(RR.at[:, s, :, :, cols], rs_recv.at[step_of(g, s)])

        def half(h):
            own = PS[s, h, block_z(0), cols].astype(F32)
            return own + RR[0, s, h, :, cols].astype(F32) + RR[1, s, h, :, cols].astype(F32)

        XS[s, :, cols] = half(1 - xh).astype(BF)
        x_copy(g, s).start()
        XO[s, :, cols] = half(xh)

    def slope(g, s):
        cols = pl.ds(*GROUPS[g])
        x_copy(g, s).wait_recv()
        slope_of(g, s, XO[s, :, cols] + XR[s, :, cols].astype(F32))
        s_copy(g, s).start()

    def slope_of(g, s, preact):
        q, cols = piece(s), pl.ds(*GROUPS[g])
        gate = jax.nn.sigmoid(preact)
        hidden = preact * gate
        cotangent = COT[rows(q * GRP, GRP), cols].astype(F32)
        SL[s, xh, block_z(0), cols] = (cotangent * gate * (1.0 + preact * (1.0 - gate))).astype(BF)
        square = hidden * hidden
        total = square[:, :128]
        for j in range(1, GROUPS[g][1] // 128):
            total += square[:, j * 128 : (j + 1) * 128]
        if g == 1:
            total += NS[s]
        NS[s] = total
        if g > 0:

            @pl.when(s == 0)
            def _():
                NR[f] = total

            @pl.when(s > 0)
            def _():
                n_copy(s).start()

    def spread_z(g, s):
        s_copy(g, s).wait_recv()
        for way in (0, 1):
            z_copy(g, s, way).start()

    def hand_on(g, s):
        drain(RR.at[:, s, :, :, pl.ds(*GROUPS[g])], z_recv.at[step_of(g, s)])
        for way in (0, 1):
            z_on(g, s, way).start()

    def gradient(g, s):
        q, cols = piece(s), pl.ds(*GROUPS[g])
        drain(XB.at[0] if g == 3 else TR.at[:, s, :, cols], on_recv.at[step_of(g, s)])

        def tile(m, _):
            here = pl.ds(pl.multiple_of(m * 256, 256), 256)
            ACC[here, cols] += lax.dot_general(
                T[q, :, :, here].reshape(8 * GRP, 256), SL[s, :, :, cols].reshape(8 * GRP, GROUPS[g][1]),
                (((0,), (0,)), ((), ())), preferred_element_type=F32,
            )
            if g >= 2:

                @pl.when(s == NF - 1)
                def _():
                    pltpu.make_async_copy(ACC.at[here], out_g.at[here], own_sem.at[4]).start()

            return 0

        lax.fori_loop(0, TC // 256, tile, 0)

    def when_in(i, run, b_run):
        b_stage = lax.rem(i + STEPS, B_EVERY) == (B_AT + SPLIT + STEPS) % B_EVERY
        full = (i >= 2 * SPLIT) & (i < STEPS)

        @pl.when((i >= 0) & (i < SPLIT))
        def _():
            run(0, i)

        @pl.when((i >= SPLIT) & (i < 2 * SPLIT))
        def _():
            run(1, i - SPLIT)

        @pl.when(full & jnp.logical_not(b_stage))
        def _():
            run(2, i - SPLIT)

        @pl.when(full & b_stage)
        def _():
            b_run(3, i - SPLIT)

    def stage(i, _):
        when_in(i, forward, forward)
        when_in(i - LAG_M, merge, b_merge)
        when_in(i - LAG_X, reduce_z, b_reduce)
        when_in(i - LAG_S, slope, b_slope)
        when_in(i - LAG_Z, spread_z, b_spread)
        when_in(i - LAG_H, hand_on, b_hand)
        tokens_on(i - SPLIT + TOKEN_LEAD)

        @pl.when(i == 0)
        def _():
            landed(partner).wait()
            for copy in second_sends:
                copy.start()

        @pl.when(i == STATES_AT)
        def _():
            drain(ST.at[1], ld_sem.at[1])
            drain(ST.at[0], ld_sem.at[2])

        @pl.when((i >= STATES_AT) & (i < STATES_AT + NF))
        def _():
            n = i - STATES_AT
            for u, old, dst in ((1, old_m, out_m), (2, old_v, out_v)):
                dy, dxl, dc = lax.rem(n + 2 * u + c, 4), lax.rem(lax.div(n, 4) + u, 2), lax.div(n, 8)
                near = jnp.where(dy == 1, 0, jnp.where(dy == 3, 1, 2))
                send_state(u, old, dst, jnp.where(dy == 0, 0, 4 + 4 * dxl + 2 * near) + 2 * dxl + dc)

        when_in(i - LAG_G, gradient, gradient)
        return 0

    lax.fori_loop(0, STEPS + LAG_G, stage, 0)

    drain(NR.at[pl.ds(0, NF - 1)], got.at[5])
    square = jnp.sum(jnp.sum(NR[...], axis=0), axis=1)
    out_n[...] = jnp.sqrt(square / FF + 1e-06)

    w_out.wait()
    own_state(1, out_m).wait()
    own_state(2, out_v).wait()
    state_wait(1, out_m)
    state_wait(2, out_v)
    others = pl.ds(0, NF - 1)
    drain(CB.at[0, others, :, pl.ds(*GROUPS[0])], sent.at[0])
    drain(CB.at[1, others], sent.at[1])
    drain(CB.at[2, others], sent.at[2])
    drain(CB.at[0, others, :, pl.ds(*GROUPS[1])], sent.at[3])
    drain(T.at[0, :, pl.ds(0, 7 * GRP // 2)], sent.at[4])
    drain(T.at[pl.ds(0, 9)], sent.at[5])
    drain(T.at[pl.ds(0, 6)], sent.at[6])
    plain, crossed = pl.ds(0, NF - NB), pl.ds(0, NB)
    drain(TR.at[:, plain], sent.at[7])
    drain(RR.at[:, plain], sent.at[8])
    drain(XS.at[plain], sent.at[9])
    drain(XS.at[plain], sent.at[10])
    drain(RR.at[:, plain], sent.at[11])
    drain(TR.at[:, plain], sent.at[12])
    drain(XB.at[crossed], sent.at[14])
    drain(TR.at[:, crossed, pl.ds(0, 16)], sent.at[15])
    drain(TR.at[:, crossed], sent.at[16])
    drain(TR.at[:, crossed], sent.at[17])
    drain(TR.at[:, crossed, pl.ds(0, 16)], sent.at[18])
    drain(XB.at[crossed], sent.at[19])
    drain(NS.at[others], sent.at[13])
    drain(ACC, own_sem.at[4])


def update_kernel(w, m, v, g, new_w, new_m, new_v):
    weight, grad = w[...].astype(F32), g[...] * SCALE
    first = 0.9 * m[...].astype(F32) + 0.1 * grad
    second = 0.95 * v[...].astype(F32) + 0.05 * grad * grad
    new_m[...] = first
    new_v[...] = second
    update = first * (1.0 / (1.0 - 0.9**10)) / (jnp.sqrt(second * (1.0 / (1.0 - 0.95**10))) + 1e-08)
    new_w[...] = weight - 0.02 * (update + 0.1 * weight)


def body(old_weight, old_first, old_second, tokens, cotangent):
    anywhere = pl.BlockSpec(memory_space=pl.ANY)
    vmem = pl.BlockSpec(memory_space=pltpu.VMEM)
    tile = jax.ShapeDtypeStruct((TC, FC), BF)
    dma = pltpu.SemaphoreType.DMA
    w, m, v, g, n = pl.pallas_call(
        step_kernel,
        out_shape=(
            tile, tile, tile,
            jax.ShapeDtypeStruct((TC, FC), F32),
            jax.ShapeDtypeStruct((GRP,), F32),
        ),
        in_specs=[anywhere] * 5,
        out_specs=(anywhere, anywhere, anywhere, anywhere, vmem),
        scratch_shapes=[
            pltpu.VMEM((NF, 2, 4 * GRP, TC), BF),
            pltpu.VMEM((TC, FC), BF),
            pltpu.VMEM((NF, 2, 4 * GRP, FC), BF),
            pltpu.VMEM((2, NF, GRP, FC), BF),
            pltpu.VMEM((2, NF, 2, GRP, FC), BF),
            pltpu.VMEM((NF, GRP, FC), F32),
            pltpu.VMEM((NF, GRP, FC), BF),
            pltpu.VMEM((NF, GRP, FC), BF),
            pltpu.VMEM((-(-NF // B_EVERY), 4 * GRP, FC), BF),
            pltpu.VMEM((NF, 2, 4 * GRP, FC), BF),
            pltpu.VMEM((TC, FC), F32),
            pltpu.VMEM((2, NF, SR, FC), F32),
            pltpu.VMEM((3, NF, SR, FC), BF),
            pltpu.VMEM((NF, GRP, 128), F32),
            pltpu.VMEM((NF, GRP, 128), F32),
            pltpu.VMEM((8 * SR, FC), BF),
            dma((3,)), dma((6,)), dma((20,)), dma((6,)), dma((NF,)),
            dma((STEPS,)), dma((STEPS,)), dma((STEPS,)), dma((STEPS,)), dma((STEPS,)), dma((STEPS,)),
        ],
        compiler_params=pltpu.CompilerParams(
            collective_id=1, has_side_effects=True, vmem_limit_bytes=60 << 20
        ),
        name="train_step",
    )(tokens, cotangent, old_weight, old_first, old_second)

    rows = UPD_ROWS
    block = pl.BlockSpec((rows, FC), lambda i: (i, 0))
    shape = jax.ShapeDtypeStruct((TC, FC), F32)
    new_weight, new_first, new_second = pl.pallas_call(
        update_kernel,
        grid=(TC // rows,),
        out_shape=(shape, shape, shape),
        in_specs=[block] * 4,
        out_specs=(block, block, block),
        compiler_params=pltpu.CompilerParams(vmem_limit_bytes=UPD_LIMIT),
        name="adamw_update",
    )(w, m, v, g)
    return new_weight, new_first, new_second, n


def solution(mesh):
    placed = (
        P(("dp", "fsdp"), None),
        P(("dp", "fsdp"), None),
        P(("dp", "fsdp"), None),
        P(("dp", "fsdp"), None),
        P("dp", "fsdp"),
    )
    return jax.shard_map(
        body,
        mesh=mesh,
        in_specs=placed,
        out_specs=(P("dp", "fsdp"), P("dp", "fsdp"), P("dp", "fsdp"), P(("dp", "fsdp"))),
        check_vma=False,
    )
```

```python
import functools

import jax
import jax.numpy as jnp
from jax import lax
from jax.experimental import pallas as pl
from jax.experimental.pallas import tpu as pltpu
from jax.sharding import PartitionSpec as P

D = 8192
FF = 14336
SCALE = D ** (-0.5)
NF = 16
NZ = 4
UPD_ROWS = 512
UPD_LIMIT = 60 << 20
GRP = 32
TC = 1024
FC = 896
SR = 64
GROUPS = ((0, 512), (512, 384), (0, 896), (0, 896))
SPLIT = 4
STEPS = NF + SPLIT
B_SET = (4, 2)
B_EVERY, B_AT = B_SET
NB = len([s for s in range(SPLIT, NF) if s % B_EVERY == B_AT])
TOKEN_LEAD = 2
LAGS = (1, 2, 3, 4, 5, 7)
LAG_M, LAG_X, LAG_S, LAG_Z, LAG_H, LAG_G = LAGS
STATES_AT = 4
MESH = pl.DeviceIdType.MESH
BF, F32 = jnp.bfloat16, jnp.float32


def step_kernel(
    tok, cot, old_w, old_m, old_v,
    out_states, out_g, out_n,
    T, W, PS, TR, RR, XO, XS, XR, XB, SL, ACC, ST, CB, NS, NR, COT,
    ld_sem, own_sem, sent, got, tk_recv, tr_recv, rs_recv, x_recv, s_recv, z_recv, on_recv,
):
    out_w, out_m, out_v = (out_states.at[j] for j in range(3))
    d, f = lax.axis_index("dp"), lax.axis_index("fsdp")
    z, xh = lax.div(d, 2), lax.rem(d, 2)
    y, xl, c = lax.div(f, 4), lax.rem(lax.div(f, 2), 2), lax.rem(f, 2)

    def at_f(dy, dxl, dc):
        return lax.rem(y + dy, 4) * 4 + lax.rem(xl + dxl, 2) * 2 + lax.rem(c + dc, 2)

    def piece(s):
        far = lax.div(jnp.maximum(s - 4, 0), 6)
        near = lax.div(lax.rem(jnp.maximum(s - 4, 0), 6), 2)
        along = 1 + 2 * near - 3 * lax.div(near, 2)
        dy = jnp.where(s < 4, 0, along)
        dxl = jnp.where(s < 4, lax.div(s, 2), far)
        return at_f(dy, dxl, lax.rem(s, 2))

    def at_d(dz, dxh):
        return lax.rem(z + dz, NZ) * 2 + lax.rem(xh + dxh, 2)

    def remote(src, dst, send, recv, dev):
        return pltpu.make_async_remote_copy(
            src_ref=src, dst_ref=dst, send_sem=send, recv_sem=recv, device_id=dev, device_id_type=MESH
        )

    def drain(ref, sem):
        pltpu.make_async_copy(ref, ref, sem).wait()

    def rows(start, size):
        return pl.ds(pl.multiple_of(start, 32), size)

    def load(old, i, k):
        cols = pl.ds(pl.multiple_of(piece(k) * FC, 128), FC)
        return pltpu.make_async_copy(old.at[:, cols], ST.at[i % 2, k], ld_sem.at[i])

    def load_all(old, i):
        def go(k, _):
            load(old, i, k).start()
            return 0

        lax.fori_loop(0, NF, go, 0)

    def state_copy(i, dst, k):
        return remote(
            CB.at[i, k], dst.at[rows(f * SR, SR)], sent.at[i], got.at[i], (d, piece(k))
        )

    def w_copy(g, k):
        cols = pl.ds(*GROUPS[g])
        return remote(
            CB.at[0, k, :, cols], W.at[rows(f * SR, SR), cols], sent.at[3 * g], got.at[3 * g], (d, piece(k))
        )

    def w_wait(g):
        drain(W.at[pl.ds(0, (NF - 1) * SR), pl.ds(*GROUPS[g])], got.at[3 * g])

    def state_wait(i, dst):
        drain(dst.at[pl.ds(0, (NF - 1) * SR)], got.at[i])

    def send_state(i, old, dst, k):
        CB[i, k] = ST[i % 2, k].astype(BF)

        @pl.when(k > 0)
        def _():
            state_copy(i, dst, k).start()

        @pl.when(k == 0)
        def _():
            own_state(i, dst).start()

    def own_state(i, dst):
        return pltpu.make_async_copy(CB.at[i, 0], dst.at[rows(f * SR, SR)], own_sem.at[i])

    load_all(old_w, 0)
    own_tokens = pltpu.make_async_copy(
        tok.at[:, pl.ds(pl.multiple_of(d * TC, 128), TC)], T.at[f, xh, rows(z * GRP, GRP)], own_sem.at[0]
    )
    own_tokens.start()
    cot_load = pltpu.make_async_copy(cot, COT, own_sem.at[5])
    cot_load.start()
    load_all(old_m, 1)

    barrier = pltpu.get_barrier_semaphore()

    def greet_f(k, _):
        pl.semaphore_signal(barrier, inc=1, device_id=(d, piece(k)), device_id_type=MESH)
        return 0

    lax.fori_loop(1, NF, greet_f, 0)

    def greet_d(k, _):
        pl.semaphore_signal(barrier, inc=1, device_id=(lax.rem(d + k, 8), f), device_id_type=MESH)
        return 0

    lax.fori_loop(1, 8, greet_d, 0)
    pl.semaphore_wait(barrier, NF - 1 + 7)

    def t1_copy(k):
        q = lax.rem(d + k, 8)
        cols = pl.ds(pl.multiple_of(q * TC, 128), TC)
        return remote(
            tok.at[:, cols], T.at[f, xh, rows(z * GRP, GRP)], sent.at[4], got.at[4], (q, f)
        )

    def t1_go(k, _):
        t1_copy(k).start()
        return 0

    lax.fori_loop(1, 8, t1_go, 0)

    drain(ST.at[0], ld_sem.at[0])

    def w_go(n, _):
        k = NF - 1 - n
        CB[0, k] = ST[0, k].astype(BF)

        @pl.when(k > 0)
        def _():
            w_copy(0, k).start()

        return 0

    lax.fori_loop(0, NF, w_go, 0)
    W[rows(f * SR, SR)] = CB[0, 0]
    load_all(old_v, 2)

    drain(T.at[0, :, pl.ds(0, 7 * GRP // 2)], got.at[4])
    own_tokens.wait()

    def token_copy(q, dev_f, kind=5):
        return remote(T.at[q], T.at[q], sent.at[kind], tk_recv.at[q], (d, dev_f))

    def landed(q):
        return pltpu.make_async_copy(T.at[q], T.at[q], tk_recv.at[q])

    sibling = at_f(0, 0, 1)
    partner = at_f(0, 1, 0)
    early_sends = [token_copy(f, partner), token_copy(f, sibling)]
    first_sends = [token_copy(f, at_f(dy, 0, 0)) for dy in (1, 3)]
    second_sends = [token_copy(partner, at_f(dy, 0, 0)) for dy in (1, 3)]
    second_sends += [token_copy(partner, sibling)]

    def y_on(dxl):
        return token_copy(at_f(3 - 2 * c, dxl, 0), at_f(1 + 2 * c, 0, 0))

    for copy in early_sends:
        copy.start()
    ACC[...] = jnp.zeros_like(ACC)
    cot_load.wait()
    w_wait(0)

    def w_rest(n, _):
        w_copy(1, NF - 1 - n).start()
        return 0

    lax.fori_loop(0, NF - 1, w_rest, 0)
    for copy in first_sends:
        copy.start()
    w_out = pltpu.make_async_copy(W, out_w, own_sem.at[3])

    def to_z(way):
        return (at_d((1, 3)[way], 0), f)

    def block_z(dz):
        return rows(lax.rem(z + dz, NZ) * GRP, GRP)

    def part_z(dz, way):
        return pl.ds(pl.multiple_of(lax.rem(z + dz, NZ) * GRP + way * 16, 16), 16)

    def step_of(g, s):
        return s if g == 0 else s + SPLIT

    def transit(g, s, way):
        cols = pl.ds(*GROUPS[g])
        return remote(
            PS.at[s, way, block_z(2), cols], TR.at[way, s, :, cols], sent.at[7], tr_recv.at[step_of(g, s)], to_z(way)
        )

    def rs_copy(g, s, way):
        cols = pl.ds(*GROUPS[g])
        return remote(
            PS.at[s, :, block_z((1, 3)[way]), cols], RR.at[way, s, :, :, cols], sent.at[8],
            rs_recv.at[step_of(g, s)], to_z(way),
        )

    def x_copy(g, s):
        cols = pl.ds(*GROUPS[g])
        return remote(XS.at[s, :, cols], XR.at[s, :, cols], sent.at[9], x_recv.at[step_of(g, s)], (at_d(0, 1), f))

    def s_copy(g, s):
        mine = SL.at[s, xh, block_z(0), pl.ds(*GROUPS[g])]
        return remote(mine, mine, sent.at[10], s_recv.at[step_of(g, s)], (at_d(0, 1), f))

    def z_copy(g, s, way):
        mine = SL.at[s, :, block_z(0), pl.ds(*GROUPS[g])]
        return remote(mine, mine, sent.at[11], z_recv.at[step_of(g, s)], to_z(way))

    def z_on(g, s, way):
        here = SL.at[s, way, block_z((3, 1)[way]), pl.ds(*GROUPS[g])]
        return remote(here, here, sent.at[12], on_recv.at[step_of(g, s)], to_z(way))

    def b_cross(s):
        return remote(
            PS.at[s, 1 - xh], XB.at[lax.div(s, B_EVERY)], sent.at[14], tr_recv.at[step_of(3, s)], (at_d(0, 1), f)
        )

    def b_transit(s, way):
        return remote(
            PS.at[s, xh, part_z(2, way)], TR.at[way, s, pl.ds(0, 16)], sent.at[15], rs_recv.at[step_of(3, s)],
            to_z(way),
        )

    def b_rs(s, way):
        return remote(
            PS.at[s, xh, block_z((1, 3)[way])], RR.at[way, s, 0], sent.at[16], x_recv.at[step_of(3, s)], to_z(way)
        )

    def b_z(s, way):
        mine = SL.at[s, xh, block_z(0)]
        return remote(mine, mine, sent.at[17], s_recv.at[step_of(3, s)], to_z(way))

    def b_on(s, way):
        here = SL.at[s, xh, part_z((3, 1)[way], way)]
        return remote(here, here, sent.at[18], z_recv.at[step_of(3, s)], to_z(way))

    def b_back(s):
        mine = SL.at[s, xh]
        return remote(mine, mine, sent.at[19], on_recv.at[step_of(3, s)], (at_d(0, 1), f))

    def n_copy(s):
        return remote(NS.at[s], NR.at[f], sent.at[13], got.at[5], (d, piece(s)))

    def tokens_on(j):
        @pl.when((lax.rem(j, 2) == 0) & (j >= 4) & (j < NF))
        def _():
            q = piece(j)
            landed(q).wait()
            token_copy(q, sibling, 6).start()

        @pl.when(j == 6)
        def _():
            y_on(0).start()

        @pl.when(j == 12)
        def _():
            y_on(1).start()

    def forward(g, s):
        q, cols = piece(s), pl.ds(*GROUPS[g])

        if g != 1:

            @pl.when(lax.rem(s, 2) == 1)
            def _():
                landed(q).wait()
        if g == 1 or SPLIT == 0:

            @pl.when(s == 0)
            def _():
                w_wait(1)
                w_out.start()

        part = jnp.dot(T[q].reshape(8 * GRP, TC), W[:, cols], preferred_element_type=F32) * SCALE
        PS[s, :, :, cols] = part.astype(BF).reshape(2, 4 * GRP, GROUPS[g][1])
        if g == 3:
            b_cross(s).start()
        else:
            for way in (0, 1):
                transit(g, s, way).start()

    def b_merge(g, s):
        drain(XB.at[0], tr_recv.at[step_of(3, s)])
        PS[s, xh] = (PS[s, xh].astype(F32) + XB[lax.div(s, B_EVERY)].astype(F32)).astype(BF)
        for way in (0, 1):
            b_transit(s, way).start()

    def b_reduce(g, s):
        drain(TR.at[:, s, pl.ds(0, 16)], rs_recv.at[step_of(3, s)])
        for way in (0, 1):
            here = part_z((1, 3)[way], way)
            PS[s, xh, here] = (PS[s, xh, here].astype(F32) + TR[way, s, pl.ds(0, 16)].astype(F32)).astype(BF)
            b_rs(s, way).start()

    def b_slope(g, s):
        drain(TR.at[:, s], x_recv.at[step_of(3, s)])
        preact = PS[s, xh, block_z(0)].astype(F32) + RR[0, s, 0].astype(F32) + RR[1, s, 0].astype(F32)
        slope_of(g, s, preact)
        for way in (0, 1):
            b_z(s, way).start()

    def b_spread(g, s):
        drain(TR.at[:, s], s_recv.at[step_of(3, s)])
        for way in (0, 1):
            b_on(s, way).start()

    def b_hand(g, s):
        drain(TR.at[:, s, pl.ds(0, 16)], z_recv.at[step_of(3, s)])
        b_back(s).start()

    def merge(g, s):
        cols = pl.ds(*GROUPS[g])
        drain(TR.at[:, s, :, cols], tr_recv.at[step_of(g, s)])
        for way in (0, 1):
            here = block_z((1, 3)[way])
            PS[s, way, here, cols] = (PS[s, way, here, cols].astype(F32) + TR[way, s, :, cols].astype(F32)).astype(BF)
            rs_copy(g, s, way).start()

    def reduce_z(g, s):
        cols = pl.ds(*GROUPS[g])
        drain(RR.at[:, s, :, :, cols], rs_recv.at[step_of(g, s)])

        def half(h):
            own = PS[s, h, block_z(0), cols].astype(F32)
            return own + RR[0, s, h, :, cols].astype(F32) + RR[1, s, h, :, cols].astype(F32)

        XS[s, :, cols] = half(1 - xh).astype(BF)
        x_copy(g, s).start()
        XO[s, :, cols] = half(xh)

    def slope(g, s):
        cols = pl.ds(*GROUPS[g])
        x_copy(g, s).wait_recv()
        slope_of(g, s, XO[s, :, cols] + XR[s, :, cols].astype(F32))
        s_copy(g, s).start()

    def slope_of(g, s, preact):
        q, cols = piece(s), pl.ds(*GROUPS[g])
        gate = jax.nn.sigmoid(preact)
        hidden = preact * gate
        cotangent = COT[rows(q * GRP, GRP), cols].astype(F32)
        SL[s, xh, block_z(0), cols] = (cotangent * gate * (1.0 + preact * (1.0 - gate))).astype(BF)
        square = hidden * hidden
        total = square[:, :128]
        for j in range(1, GROUPS[g][1] // 128):
            total += square[:, j * 128 : (j + 1) * 128]
        if g == 1:
            total += NS[s]
        NS[s] = total
        if g > 0:

            @pl.when(s == 0)
            def _():
                NR[f] = total

            @pl.when(s > 0)
            def _():
                n_copy(s).start()

    def spread_z(g, s):
        s_copy(g, s).wait_recv()
        for way in (0, 1):
            z_copy(g, s, way).start()

    def hand_on(g, s):
        drain(RR.at[:, s, :, :, pl.ds(*GROUPS[g])], z_recv.at[step_of(g, s)])
        for way in (0, 1):
            z_on(g, s, way).start()

    def gradient(g, s):
        q, cols = piece(s), pl.ds(*GROUPS[g])
        drain(XB.at[0] if g == 3 else TR.at[:, s, :, cols], on_recv.at[step_of(g, s)])

        def tile(m, _):
            here = pl.ds(pl.multiple_of(m * 256, 256), 256)
            ACC[here, cols] += lax.dot_general(
                T[q, :, :, here].reshape(8 * GRP, 256), SL[s, :, :, cols].reshape(8 * GRP, GROUPS[g][1]),
                (((0,), (0,)), ((), ())), preferred_element_type=F32,
            )
            if g >= 2:

                @pl.when(s == NF - 1)
                def _():
                    pltpu.make_async_copy(ACC.at[here], out_g.at[here], own_sem.at[4]).start()

            return 0

        lax.fori_loop(0, TC // 256, tile, 0)

    def when_in(i, run, b_run):
        b_stage = lax.rem(i + STEPS, B_EVERY) == (B_AT + SPLIT + STEPS) % B_EVERY
        full = (i >= 2 * SPLIT) & (i < STEPS)

        @pl.when((i >= 0) & (i < SPLIT))
        def _():
            run(0, i)

        @pl.when((i >= SPLIT) & (i < 2 * SPLIT))
        def _():
            run(1, i - SPLIT)

        @pl.when(full & jnp.logical_not(b_stage))
        def _():
            run(2, i - SPLIT)

        @pl.when(full & b_stage)
        def _():
            b_run(3, i - SPLIT)

    def stage(i, _):
        when_in(i, forward, forward)
        when_in(i - LAG_M, merge, b_merge)
        when_in(i - LAG_X, reduce_z, b_reduce)
        when_in(i - LAG_S, slope, b_slope)
        when_in(i - LAG_Z, spread_z, b_spread)
        when_in(i - LAG_H, hand_on, b_hand)
        tokens_on(i - SPLIT + TOKEN_LEAD)

        @pl.when(i == 0)
        def _():
            landed(partner).wait()
            for copy in second_sends:
                copy.start()

        @pl.when(i == STATES_AT)
        def _():
            drain(ST.at[1], ld_sem.at[1])
            drain(ST.at[0], ld_sem.at[2])

        @pl.when((i >= STATES_AT) & (i < STATES_AT + NF))
        def _():
            n = i - STATES_AT
            for u, old, dst in ((1, old_m, out_m), (2, old_v, out_v)):
                dy, dxl, dc = lax.rem(n + 2 * u + c, 4), lax.rem(lax.div(n, 4) + u, 2), lax.div(n, 8)
                near = jnp.where(dy == 1, 0, jnp.where(dy == 3, 1, 2))
                send_state(u, old, dst, jnp.where(dy == 0, 0, 4 + 4 * dxl + 2 * near) + 2 * dxl + dc)

        when_in(i - LAG_G, gradient, gradient)
        return 0

    lax.fori_loop(0, STEPS + LAG_G, stage, 0)

    drain(NR.at[pl.ds(0, NF - 1)], got.at[5])
    square = jnp.sum(jnp.sum(NR[...], axis=0), axis=1)
    out_n[...] = jnp.sqrt(square / FF + 1e-06)

    w_out.wait()
    own_state(1, out_m).wait()
    own_state(2, out_v).wait()
    state_wait(1, out_m)
    state_wait(2, out_v)
    others = pl.ds(0, NF - 1)
    drain(CB.at[0, others, :, pl.ds(*GROUPS[0])], sent.at[0])
    drain(CB.at[1, others], sent.at[1])
    drain(CB.at[2, others], sent.at[2])
    drain(CB.at[0, others, :, pl.ds(*GROUPS[1])], sent.at[3])
    drain(T.at[0, :, pl.ds(0, 7 * GRP // 2)], sent.at[4])
    drain(T.at[pl.ds(0, 9)], sent.at[5])
    drain(T.at[pl.ds(0, 6)], sent.at[6])
    plain, crossed = pl.ds(0, NF - NB), pl.ds(0, NB)
    drain(TR.at[:, plain], sent.at[7])
    drain(RR.at[:, plain], sent.at[8])
    drain(XS.at[plain], sent.at[9])
    drain(XS.at[plain], sent.at[10])
    drain(RR.at[:, plain], sent.at[11])
    drain(TR.at[:, plain], sent.at[12])
    drain(XB.at[crossed], sent.at[14])
    drain(TR.at[:, crossed, pl.ds(0, 16)], sent.at[15])
    drain(TR.at[:, crossed], sent.at[16])
    drain(TR.at[:, crossed], sent.at[17])
    drain(TR.at[:, crossed, pl.ds(0, 16)], sent.at[18])
    drain(XB.at[crossed], sent.at[19])
    drain(NS.at[others], sent.at[13])
    drain(ACC, own_sem.at[4])


def update_kernel(states, g, new_w, new_m, new_v):
    weight, grad = states[0].astype(F32), g[...] * SCALE
    first = 0.9 * states[1].astype(F32) + 0.1 * grad
    second = 0.95 * states[2].astype(F32) + 0.05 * grad * grad
    new_m[...] = first
    new_v[...] = second
    update = first * (1.0 / (1.0 - 0.9**10)) / (jnp.sqrt(second * (1.0 / (1.0 - 0.95**10))) + 1e-08)
    new_w[...] = weight - 0.02 * (update + 0.1 * weight)


def body(old_weight, old_first, old_second, tokens, cotangent):
    anywhere = pl.BlockSpec(memory_space=pl.ANY)
    vmem = pl.BlockSpec(memory_space=pltpu.VMEM)
    dma = pltpu.SemaphoreType.DMA
    states, g, n = pl.pallas_call(
        step_kernel,
        out_shape=(
            jax.ShapeDtypeStruct((3, TC, FC), BF),
            jax.ShapeDtypeStruct((TC, FC), F32),
            jax.ShapeDtypeStruct((GRP,), F32),
        ),
        in_specs=[anywhere] * 5,
        out_specs=(anywhere, anywhere, vmem),
        scratch_shapes=[
            pltpu.VMEM((NF, 2, 4 * GRP, TC), BF),
            pltpu.VMEM((TC, FC), BF),
            pltpu.VMEM((NF, 2, 4 * GRP, FC), BF),
            pltpu.VMEM((2, NF, GRP, FC), BF),
            pltpu.VMEM((2, NF, 2, GRP, FC), BF),
            pltpu.VMEM((NF, GRP, FC), F32),
            pltpu.VMEM((NF, GRP, FC), BF),
            pltpu.VMEM((NF, GRP, FC), BF),
            pltpu.VMEM((-(-NF // B_EVERY), 4 * GRP, FC), BF),
            pltpu.VMEM((NF, 2, 4 * GRP, FC), BF),
            pltpu.VMEM((TC, FC), F32),
            pltpu.VMEM((2, NF, SR, FC), F32),
            pltpu.VMEM((3, NF, SR, FC), BF),
            pltpu.VMEM((NF, GRP, 128), F32),
            pltpu.VMEM((NF, GRP, 128), F32),
            pltpu.VMEM((8 * SR, FC), BF),
            dma((3,)), dma((6,)), dma((20,)), dma((6,)), dma((NF,)),
            dma((STEPS,)), dma((STEPS,)), dma((STEPS,)), dma((STEPS,)), dma((STEPS,)), dma((STEPS,)),
        ],
        compiler_params=pltpu.CompilerParams(
            collective_id=1, has_side_effects=True, vmem_limit_bytes=60 << 20
        ),
        name="train_step",
    )(tokens, cotangent, old_weight, old_first, old_second)

    rows = UPD_ROWS
    block = pl.BlockSpec((rows, FC), lambda i: (i, 0))
    shape = jax.ShapeDtypeStruct((TC, FC), F32)
    new_weight, new_first, new_second = pl.pallas_call(
        update_kernel,
        grid=(TC // rows,),
        out_shape=(shape, shape, shape),
        in_specs=[pl.BlockSpec((3, rows, FC), lambda i: (0, i, 0)), block],
        out_specs=(block, block, block),
        compiler_params=pltpu.CompilerParams(vmem_limit_bytes=UPD_LIMIT),
        name="adamw_update",
    )(states, g)
    return new_weight, new_first, new_second, n


def solution(mesh):
    placed = (
        P(("dp", "fsdp"), None),
        P(("dp", "fsdp"), None),
        P(("dp", "fsdp"), None),
        P(("dp", "fsdp"), None),
        P("dp", "fsdp"),
    )
    return jax.shard_map(
        body,
        mesh=mesh,
        in_specs=placed,
        out_specs=(P("dp", "fsdp"), P("dp", "fsdp"), P("dp", "fsdp"), P(("dp", "fsdp"))),
        check_vma=False,
    )
```
